512 devices in a mesh: blk: 128 (over y, x, z_lo, core), pitch: 4 (over z_hi).
Axes of the slice: x: 4, y: 8, z: 8 (z_hi: 4, z_lo: 2; z = z_hi * 2 + z_lo), core: 2. Of those that a mesh axis runs over, the one named last changes fastest.
Arguments:
- flow_state: float32 [5, 32, 2048, 128], P(None, 'pitch', 'blk'), may hold values from -0.6 to 3.2, as said below
- prior_state: float32 [5, 32, 2048, 128], P(None, 'pitch', 'blk'), may hold values from -0.75 to 3.35, as said below
- fourier_store: float32 [2, 49, 10, 2048, 128], P(None, None, None, ('blk', 'pitch')), may hold values from -0.15 to 2.6, as said below
- sample_times: int32 [2, 2048, 128], P(None, ('blk', 'pitch')), may hold values from 0 to 95
- harmonics: int32 [2048, 128], P(('blk', 'pitch')), may hold values from 12 to 24
Outputs:
- new_state: float32 [5, 32, 2048, 128], P(None, 'pitch', 'blk')
- new_store: float32 [2, 49, 10, 2048, 128], P(None, None, None, ('blk', 'pitch'))
- new_ghosts: float32 [2, 10, 2048, 128], P(None, None, ('blk', 'pitch'))
The draws below stay inside these ranges and needn't reach their ends.
Inputs may be any that keep to these rules, and one draw needn't show every extreme that they name: `flow_state`: density between 0.7 and 1.3, momenta between -0.6 and 0.6, total energy between 2.2 and 3.2. `prior_state`: each entry within 0.15 of flow_state's. `fourier_store`: the k-th cosine and sine coefficients are at most 0.08 / k in magnitude.
All inputs are finite; a program needn't handle non-finite values.
Results may differ from the reference program's by a relative error of at most 0.000068.
Values sent between devices are 32-bit elements; how exact they have to be, the bound alone decides.
A program may use at most 64 MiB of HBM per device.

```python
import math
import jax
import jax.numpy as jnp
from jax import lax

CR = 128
HARM = 24
NT = 96
NP = 32
NA = 2048


def base_state(key):
    shape = (NP, NA, CR)
    keys = jax.random.split(key, 5)
    density = jax.random.uniform(keys[0], shape, jnp.float32, 0.8, 1.2)
    moments = [jax.random.uniform(keys[1 + which], shape, jnp.float32, -0.5, 0.5) for which in range(3)]
    energy = jax.random.uniform(keys[4], shape, jnp.float32, 2.3, 3.1)
    return jnp.stack([density, moments[0], moments[1], moments[2], energy])


def draw_flow_state(key, part):
    return base_state(jax.random.fold_in(key, 11))


def draw_prior_state(key, part):
    offsets = jax.random.uniform(jax.random.fold_in(key, 12), (5, NP, NA, CR), jnp.float32, -0.15, 0.15)
    return base_state(jax.random.fold_in(key, 11)) + offsets


def draw_fourier_store(key, part):
    first, second = jax.random.split(jax.random.fold_in(key, 21))
    levels = jnp.array([1.0, 1.0, 0.0, 0.0, 0.0, 0.0, 0.0, 0.0, 2.5, 2.5], jnp.float32).reshape((1, 1, 10, 1, 1))
    orders = jnp.arange(1, HARM + 1).astype(jnp.float32)
    spread = 0.1
    weights = 0.08 / jnp.concatenate([orders, orders])
    mean_part = levels + spread * jax.random.uniform(first, (2, 1, 10, NA, CR), jnp.float32, -1.0, 1.0)
    harm_part = jax.random.uniform(second, (2, 2 * HARM, 10, NA, CR), jnp.float32, -1.0, 1.0) * weights.reshape((1, 2 * HARM, 1, 1, 1))
    return jnp.concatenate([mean_part, harm_part], axis=1)


def place_ends(values, stream_key, smallest, high):
    spot = [jax.random.randint(jax.random.fold_in(stream_key, axis), (), 0, length) for axis, length in enumerate(values.shape)]
    main_axis = values.shape.index(max(values.shape))
    neighbour = spot[:main_axis] + [(spot[main_axis] + 1) % values.shape[main_axis]] + spot[main_axis + 1:]
    return values.at[tuple(spot)].set(smallest).at[tuple(neighbour)].set(high)


def setup_inputs(seed: int = 0) -> dict:
    key_list = jax.random.split(jax.random.key(seed), 6)
    return {
        "flow_state": draw_flow_state(jax.random.fold_in(key_list[5], 71), 0),
        "prior_state": draw_prior_state(jax.random.fold_in(key_list[5], 71), 0),
        "fourier_store": draw_fourier_store(jax.random.fold_in(key_list[5], 71), 0),
        "sample_times": place_ends(jax.random.randint(key_list[3], (2, NA, CR), 0, NT), jax.random.fold_in(key_list[3], 1), 0, NT - 1).astype(jnp.int32),
        "harmonics": place_ends(jax.random.randint(key_list[4], (NA, CR), HARM // 2, HARM + 1), jax.random.fold_in(key_list[4], 1), HARM // 2, HARM).astype(jnp.int32),
    }


gamma_less = 0.4
diss_coeff = 0.03125
section_coefs = (1.0 / 3.0, 0.5, 1.0)
pseudo_step = 0.1
physical_step = 0.25
relax_rate = 0.125
lag_turns = 0.3


def fluxes(current, direction):
    density = current[0]
    velocity = current[direction] / density
    pressure = gamma_less * (current[4] - 0.5 * (current[1] * current[1] + current[2] * current[2] + current[3] * current[3]) / density)
    flux_parts = [current[direction], current[1] * velocity, current[2] * velocity, current[3] * velocity, (current[4] + pressure) * velocity]
    flux_parts[direction] = flux_parts[direction] + pressure
    return jnp.stack(flux_parts)


def face_sum(padded, direction):
    cells_n = padded.shape[direction] - 4
    faces_n = cells_n + 1
    cell_flux = fluxes(padded, direction)

    def window(values, offset, length):
        return lax.slice_in_dim(values, offset, offset + length, axis=direction)

    face_flux = 0.5 * (window(cell_flux, 1, faces_n) + window(cell_flux, 2, faces_n)) - diss_coeff * (window(padded, 3, faces_n) - 3.0 * window(padded, 2, faces_n) + 3.0 * window(padded, 1, faces_n) - window(padded, 0, faces_n))
    return window(face_flux, 1, cells_n) - window(face_flux, 0, cells_n)


def harmonic_tables(phases_at, harm_count):
    orders = jnp.arange(1, harm_count + 1).astype(jnp.float32).reshape((harm_count, 1, 1))
    angles = orders * phases_at[None]
    return jnp.cos(angles), jnp.sin(angles)


def rebuild(coeffs, phases_at, active):
    harm_count = (coeffs.shape[0] - 1) // 2
    cosines, sines = harmonic_tables(phases_at, harm_count)
    orders = jnp.arange(1, harm_count + 1).astype(jnp.int32).reshape((harm_count, 1, 1))
    active_mask = (orders <= active[None]).astype(jnp.float32)
    harm_terms = coeffs[1:harm_count + 1] * (active_mask * cosines)[:, None] + coeffs[harm_count + 1:] * (active_mask * sines)[:, None]
    return coeffs[0] + jnp.sum(harm_terms, axis=0)


def refresh(coeffs, samples, phases_at):
    harm_count = (coeffs.shape[0] - 1) // 2
    cosines, sines = harmonic_tables(phases_at, harm_count)
    mean_part = (1.0 - relax_rate) * coeffs[0] + relax_rate * samples
    cos_part = (1.0 - relax_rate) * coeffs[1:harm_count + 1] + (2.0 * relax_rate) * samples[None] * cosines[:, None]
    sin_part = (1.0 - relax_rate) * coeffs[harm_count + 1:] + (2.0 * relax_rate) * samples[None] * sines[:, None]
    return jnp.concatenate([mean_part[None], cos_part, sin_part], axis=0)


def residual(current, flow_state, prior_state, low_ghost, high_ghost):
    pitch_pad = jnp.concatenate([low_ghost, current, high_ghost], axis=1)
    axial_pad = jnp.pad(current, ((0, 0), (0, 0), (2, 2), (0, 0)), mode="edge")
    radial_pad = jnp.pad(current, ((0, 0), (0, 0), (0, 0), (2, 2)), mode="edge")
    summed = face_sum(pitch_pad, 1) + face_sum(axial_pad, 2) + face_sum(radial_pad, 3)
    return summed + (3.0 * current - 4.0 * flow_state + prior_state) * (0.5 / physical_step)


def reference(flow_state, prior_state, fourier_store, sample_times, harmonics):
    period = 2.0 * math.pi / NT
    phase_lag = 2.0 * math.pi * lag_turns
    phases = sample_times.astype(jnp.float32) * period
    ghost_shape = (5, 2) + harmonics.shape
    low_ghost = rebuild(fourier_store[0], phases[0] - phase_lag, harmonics).reshape(ghost_shape)
    high_ghost = rebuild(fourier_store[1], phases[1] + phase_lag, harmonics).reshape(ghost_shape)
    current = flow_state
    for section_coef in section_coefs:
        current = flow_state - (section_coef * pseudo_step) * residual(current, flow_state, prior_state, low_ghost, high_ghost)
    next_phases = phases + period
    face_shape = (10,) + harmonics.shape
    low_store = refresh(fourier_store[0], current[:, -2:].reshape(face_shape), next_phases[0])
    high_store = refresh(fourier_store[1], current[:, :2].reshape(face_shape), next_phases[1])
    ghosts = jnp.stack([rebuild(low_store, next_phases[0] - phase_lag, harmonics), rebuild(high_store, next_phases[1] + phase_lag, harmonics)])
    return current, jnp.stack([low_store, high_store]), ghosts
```

```python
import functools
import math

import jax
import jax.numpy as jnp
from jax import lax
from jax.experimental import pallas as pl
from jax.experimental.pallas import tpu as pltpu
from jax.sharding import PartitionSpec as P

MESH = pl.DeviceIdType.MESH
F32 = jnp.float32
NT = 96
HARM = 24
COEFS = 2 * HARM + 1
PERIOD = 2.0 * math.pi / NT
LAG = 2.0 * math.pi * 0.3
SECTIONS = (1.0 / 3.0, 0.5, 1.0)
CENTER = (8, 16)
EXTENDED = (4, 12, 20)


def twice(ref):
    rows = ref[...]
    return jnp.concatenate([rows, rows], axis=0)


def base_turn(times):
    quarter = (times - NT // 2).astype(F32) * (PERIOD / 4.0)
    sq = quarter * quarter
    s = quarter * (1.0 + sq * (-1.0 / 6 + sq * (1.0 / 120 + sq * (-1.0 / 5040 + sq * (1.0 / 362880)))))
    c = 1.0 + sq * (
        -0.5 + sq * (1.0 / 24 + sq * (-1.0 / 720 + sq * (1.0 / 40320 + sq * (-1.0 / 3628800))))
    )
    for _ in range(2):
        c, s = 1.0 - 2.0 * s * s, 2.0 * s * c
    return -c, -s


def turned(turn, angle):
    c, s = turn
    ca, sa = math.cos(angle), math.sin(angle)
    return c * ca - s * sa, s * ca + c * sa


def times_turn(a, b):
    return a[0] * b[0] - a[1] * b[1], a[1] * b[0] + a[0] * b[1]


def half_flux(cell, direction):
    rho, mp, ma, mr, energy = cell
    half_inv = 0.5 / rho
    kinetic = (mp * mp + ma * ma + mr * mr) * half_inv
    half_p = 0.2 * (energy - kinetic)
    moment = cell[direction]
    half_u = moment * half_inv
    parts = [
        0.5 * moment,
        mp * half_u,
        ma * half_u,
        mr * half_u,
        (energy + (half_p + half_p)) * half_u,
    ]
    parts[direction] = parts[direction] + half_p
    return parts


def section(s, cur, flow, prior, out, out_offsets, first, count, rows):
    step = 0.1 * SECTIONS[s]
    lane = lax.broadcasted_iota(jnp.int32, (8, 128), 1)
    at_low, at_high = lane == 0, lane == 127

    def after(x):
        return jnp.where(at_high, x, pltpu.roll(x, 127, 1))

    def before(x):
        return jnp.where(at_low, x, pltpu.roll(x, 1, 1))

    def layer(i, carry):
        at = first + i
        li = at + 2
        for r0 in rows:

            def load(dl, dr):
                return [cur[v, li + dl, r0 + dr : r0 + dr + 8, :] for v in range(5)]

            mid = load(0, 0)
            near = [load(1, 0), load(-1, 0), load(0, 1), load(0, -1)]
            far = [load(2, 0), load(-2, 0), load(0, 2), load(0, -2)]
            fluxes = [half_flux(near[k], 1 + k // 2) for k in range(4)]
            radial = half_flux(mid, 3)
            for v in range(5):
                total = (fluxes[0][v] - fluxes[1][v]) + (fluxes[2][v] - fluxes[3][v])
                n1 = (near[0][v] + near[1][v]) + (near[2][v] + near[3][v])
                n2 = (far[0][v] + far[1][v]) + (far[2][v] + far[3][v])
                x = mid[v]
                eighth = 0.125 * x
                up = (eighth + radial[v]) - 0.03125 * after(x)
                down = (eighth - radial[v]) - 0.03125 * before(x)
                total = total + (after(up) + before(down)) + (0.125 * n1 - 0.03125 * n2)
                base = (1.0 + 8.0 * step) * flow[v, li, r0 : r0 + 8, :] - (
                    2.0 * step
                ) * prior[v, at, r0 : r0 + 8, :]
                new = base - (6.0 - 0.5625) * step * x - step * total
                out[v, at + out_offsets[0], r0 + out_offsets[1] : r0 + out_offsets[1] + 8, :] = new
        return carry

    lax.fori_loop(0, count, layer, 0)


def sections_kernel(
    flow_hbm, prior_hbm, store_hbm, times_hbm, harm_hbm,
    state_out, samples_out,
    u0, u1, u2, prior, store, times, harm, share, ghosts,
    pack, land, faces, samples,
    local_sem, send_sem, recv_sem, ready_sem,
):
    p = lax.axis_index("pitch")
    b = lax.axis_index("blk")
    n_blk = lax.axis_size("blk")
    n_pitch = lax.axis_size("pitch")
    first_p, last_p = p == 0, p == n_pitch - 1
    is_end = jnp.logical_or(first_p, last_p)
    b_low, b_high = b > 0, b < n_blk - 1
    pitch_up = {"pitch": lax.rem(p + 1, n_pitch)}
    pitch_down = {"pitch": lax.rem(p + n_pitch - 1, n_pitch)}
    states = (u0, u1, u2)

    barrier = pltpu.get_barrier_semaphore()
    for where in (pitch_up, pitch_down):
        pl.semaphore_signal(barrier, inc=1, device_id=where, device_id_type=MESH)
    for where, cond in (({"blk": b - 1}, b_low), ({"blk": b + 1}, b_high)):

        @pl.when(cond)
        def _():
            pl.semaphore_signal(barrier, inc=1, device_id=where, device_id_type=MESH)

    loads = [
        pltpu.make_async_copy(flow_hbm, u0.at[:, 2:10, 8:24, :], local_sem.at[0]),
        pltpu.make_async_copy(store_hbm.at[0], store.at[0], local_sem.at[1]),
        pltpu.make_async_copy(store_hbm.at[1], store.at[1], local_sem.at[2]),
        pltpu.make_async_copy(prior_hbm, prior.at[:, :, 8:24, :], local_sem.at[3]),
        pltpu.make_async_copy(times_hbm, times, local_sem.at[4]),
        pltpu.make_async_copy(harm_hbm, harm, local_sem.at[5]),
    ]
    for k in (0, 4, 5, 1, 2, 3):
        loads[k].start()

    pl.semaphore_wait(barrier, 2 + b_low.astype(jnp.int32) + b_high.astype(jnp.int32))

    sent = []
    counter = [0]

    def remote(src, dst, where, send_if, recv_if):
        k = counter[0]
        counter[0] += 1
        copy = pltpu.make_async_remote_copy(
            src_ref=src,
            dst_ref=dst,
            send_sem=send_sem.at[k],
            recv_sem=recv_sem.at[k],
            device_id=where,
            device_id_type=MESH,
        )
        return copy, send_if, recv_if

    def send(*copies):
        for copy, send_if, _ in copies:
            sent.append((copy, send_if))

            @pl.when(send_if)
            def _():
                copy.start()

    def arrive(*copies):
        for copy, _, recv_if in copies:

            @pl.when(recv_if)
            def _():
                copy.wait_recv()

    not_first, not_last = p > 0, p < n_pitch - 1

    def pitch_pair(src, offset, target):
        return (
            remote(
                src.at[:, offset + 6 : offset + 8, 8 * (offset // 2) : 8 * (offset // 2) + 16, :],
                target.at[:, 0:2, 8:24, :], pitch_up, not_last, not_first,
            ),
            remote(
                src.at[:, offset : offset + 2, 8 * (offset // 2) : 8 * (offset // 2) + 16, :],
                target.at[:, 10:12, 8:24, :], pitch_down, not_first, not_last,
            ),
        )

    pitch = [pitch_pair(flow_hbm, 0, u0), pitch_pair(u1, 2, u1), pitch_pair(u2, 2, u2)]
    send(*pitch[0])

    g4 = jnp.where(first_p, 0, 4)
    up_ok, down_ok = jnp.logical_and(is_end, b_high), jnp.logical_and(is_end, b_low)
    wide = [
        remote(
            flow_hbm.at[:, pl.ds(g4, 4), 8:16, :], u0.at[:, pl.ds(2 + g4, 4), 0:8, :],
            {"blk": b + 1}, up_ok, down_ok,
        ),
        remote(
            flow_hbm.at[:, pl.ds(g4, 4), 0:8, :], u0.at[:, pl.ds(2 + g4, 4), 24:32, :],
            {"blk": b - 1}, down_ok, up_ok,
        ),
        remote(
            prior_hbm.at[:, pl.ds(g4, 4), 8:16, :], prior.at[:, pl.ds(g4, 4), 0:8, :],
            {"blk": b + 1}, up_ok, down_ok,
        ),
        remote(
            prior_hbm.at[:, pl.ds(g4, 4), 0:8, :], prior.at[:, pl.ds(g4, 4), 24:32, :],
            {"blk": b - 1}, down_ok, up_ok,
        ),
    ]

    for k, where in enumerate((pitch_up, pitch_down)):
        pl.semaphore_signal(ready_sem.at[k], inc=1, device_id=where, device_id_type=MESH)

    parts = ((2, 3, 4, 5), (0, 1, 6, 7))
    axial = [
        [
            (
                remote(pack.at[s, part, 0], land.at[s, part, 0], {"blk": b + 1}, b_high, b_low),
                remote(pack.at[s, part, 1], land.at[s, part, 1], {"blk": b - 1}, b_low, b_high),
            )
            for part in range(2)
        ]
        for s in range(3)
    ]

    def axial_send(s, part):
        for side, row in ((0, 22), (1, 8)):
            for v in range(5):
                for k, at in enumerate(parts[part]):
                    pack[s, part, side, v, 2 * k : 2 * k + 2, :] = states[s][
                        v, 2 + at, row : row + 2, :
                    ]
        send(*axial[s][part])

    def axial_take(s, part):
        for side, row, cond in ((0, 6, b_low), (1, 24, b_high)):

            @pl.when(cond)
            def _():
                axial[s][part][side][0].wait_recv()
                for v in range(5):
                    for k, at in enumerate(parts[part]):
                        states[s][v, 2 + at, row : row + 2, :] = land[
                            s, part, side, v, 2 * k : 2 * k + 2, :
                        ]

    def fill_edges(s, first, count):
        ref = states[s]
        for cond, row, source in ((b == 0, 6, 8), (b == n_blk - 1, 24, 23)):

            @pl.when(cond)
            def _():
                def layer(i, carry):
                    for v in range(5):
                        edge = ref[v, 2 + first + i, source : source + 1, :]
                        ref[v, 2 + first + i, row : row + 2, :] = jnp.broadcast_to(edge, (2, 128))
                    return carry

                lax.fori_loop(0, count, layer, 0)

    loads[0].wait()
    axial_send(0, 0)
    axial_send(0, 1)
    send(*wide)

    for k in (4, 5):
        loads[k].wait()
    count8 = twice(harm)
    for x in range(2):
        loads[1 + x].wait()
        turn = turned(base_turn(twice(times.at[x])), LAG if x else -LAG)

        def harmonic(k, carry):
            now, total = carry
            keep = k <= count8
            c, s = jnp.where(keep, now[0], 0.0), jnp.where(keep, now[1], 0.0)
            total = tuple(
                total[j]
                + (
                    store[x, k, 8 * j : 8 * j + 8, :] * c
                    + store[x, HARM + k, 8 * j : 8 * j + 8, :] * s
                )
                for j in range(5)
            )
            return times_turn(now, turn), total

        start = tuple(store[x, 0, 8 * j : 8 * j + 8, :] for j in range(5))
        _, total = lax.fori_loop(1, HARM + 1, harmonic, (turn, start))
        for j in range(5):
            share[x, 8 * j : 8 * j + 8, :] = total[j]

    for k in range(2):
        pl.semaphore_wait(ready_sem.at[k], 1)

    ghost_copies = []
    for j in range(4):
        for x, target in ((0, 0), (1, 3)):
            if j != target:
                ghost_copies.append(
                    (
                        j,
                        x,
                        remote(
                            share.at[x], ghosts.at[1 + j], {"pitch": target},
                            p == j, p == target,
                        ),
                    )
                )
    beside = []
    for x, target in ((0, 0), (1, 3)):
        beside.append(
            remote(
                share.at[x], ghosts.at[0], {"blk": b + 1, "pitch": target},
                jnp.logical_and(last_p, b_high), jnp.logical_and(p == target, b_low),
            )
        )
        beside.append(
            remote(
                share.at[x], ghosts.at[5], {"blk": b - 1, "pitch": target},
                jnp.logical_and(first_p, b_low), jnp.logical_and(p == target, b_high),
            )
        )
    ghost_copies = [c[2] for c in ghost_copies] + beside
    send(*ghost_copies)
    for x, cond, slot in ((0, first_p, 1), (1, last_p, 4)):

        @pl.when(cond)
        def _():
            ghosts[slot] = share[x]

    def inner(s):
        fill_edges(s, 0, 8)
        if s < 2:
            section(s, states[s], u0, prior, states[s + 1], (2, 0), 2, 4, CENTER)
        else:
            section(s, states[s], u0, prior, state_out, (0, -8), 2, 4, CENTER)

    def pair(s, first):
        if s < 2:
            section(s, states[s], u0, prior, states[s + 1], (2, 0), first, 2, CENTER)
        else:
            section(s, states[s], u0, prior, state_out, (0, -8), first, 2, CENTER)

    def outer(s):
        for side, cond, first in ((1, not_last, 6), (0, not_first, 0)):

            @pl.when(cond)
            def _():
                pitch[s][side][0].wait_recv()
                pair(s, first)
                if s < 2:
                    pitch[s + 1][1 - side][0].start()

        if s < 2:
            sent.extend((c[0], c[1]) for c in pitch[s + 1])

    loads[3].wait()
    arrive(*wide[:2])
    axial_take(0, 0)
    axial_take(0, 1)
    inner(0)
    axial_send(1, 0)
    outer(0)
    axial_send(1, 1)

    face_copies = []
    for x, source in ((0, 3), (1, 0)):
        for j in range(4):
            if j != source:
                face_copies.append(
                    remote(faces.at[j], samples.at[x], {"pitch": j}, p == source, p == j)
                )

    @pl.when(is_end)
    def _():
        arrive(*wide[2:])
        arrive(*ghost_copies)
        g2 = jnp.where(first_p, 0, 10)
        for k in range(6):

            @pl.when(jnp.logical_or(jnp.logical_and(k > 0, k < 5), b_low if k == 0 else b_high))
            def _():
                for v in range(5):
                    for layer in range(2):
                        at = (2 * v + layer) * 4
                        block = ghosts[k, at : at + 4, :]
                        for ref in states:
                            ref[v, g2 + layer, 4 + 4 * k : 8 + 4 * k, :] = block

        near = jnp.where(first_p, 0, 6)
        beyond = jnp.where(first_p, 2, 4)
        section(0, u0, u0, prior, u1, (2, 0), near, 2, EXTENDED)
        section(0, u0, u0, prior, u1, (2, 0), beyond, 2, EXTENDED)
        fill_edges(1, g4, 4)
        section(1, u1, u0, prior, u2, (2, 0), near, 2, EXTENDED)
        section(1, u1, u0, prior, u2, (2, 0), beyond, 2, CENTER)
        fill_edges(2, g4, 4)
        section(2, u2, u0, prior, state_out, (0, -8), near, 2, CENTER)
        for j in range(4):
            for v in range(5):
                for layer in range(2):
                    at = (2 * v + layer) * 4
                    faces[j, at : at + 4, :] = state_out[v, near + layer, 4 * j : 4 * j + 4, :]

    send(*face_copies)
    for x, cond, slot in ((1, first_p, 0), (0, last_p, 3)):

        @pl.when(cond)
        def _():
            samples[x] = faces[slot]

    for s in (1, 2):
        axial_take(s, 0)
        axial_take(s, 1)
        inner(s)
        if s == 1:
            axial_send(2, 0)
        outer(s)
        if s == 1:
            axial_send(2, 1)

    arrive(*face_copies)
    samples_out[...] = samples[...]
    for copy, cond in sent:

        @pl.when(cond)
        def _():
            copy.wait_send()


GROUPS = 4


def store_kernel(
    store_hbm, times_ref, harm_ref, samples, state, store_out, ghosts_out, state_out,
    store, fresh, in_sem, out_sem,
):
    per = HARM // GROUPS
    fetch, write = {}, {}
    for x in range(2):
        for g in range(GROUPS):
            for half in range(2):
                at = 1 + HARM * half + per * g
                rows, k = pl.ds(at, per), (x * GROUPS + g) * 2 + half
                fetch[x, g, half] = pltpu.make_async_copy(
                    store_hbm.at[x, rows], store.at[x, rows], in_sem.at[k]
                )
                write[x, g, half] = pltpu.make_async_copy(
                    fresh.at[x, rows], store_out.at[x, rows], out_sem.at[k]
                )
        fetch[x, 0, 2] = pltpu.make_async_copy(
            store_hbm.at[x, 0], store.at[x, 0], in_sem.at[4 * GROUPS + x]
        )
        write[x, 0, 2] = pltpu.make_async_copy(
            fresh.at[x, 0], store_out.at[x, 0], out_sem.at[4 * GROUPS + x]
        )
    for x in range(2):
        fetch[x, 0, 2].start()
        for g in range(GROUPS):
            for half in range(2):
                fetch[x, g, half].start()
    state_copy = pltpu.make_async_copy(state, state_out, out_sem.at[4 * GROUPS + 2])
    state_copy.start()
    count8 = twice(harm_ref)
    for x in range(2):
        turn = turned(base_turn(twice(times_ref.at[x])), PERIOD)
        lagged = turned(turn, LAG if x else -LAG)
        seen = tuple(samples[x, 8 * j : 8 * j + 8, :] for j in range(5))
        fetch[x, 0, 2].wait()
        total = tuple(
            0.875 * store[x, 0, 8 * j : 8 * j + 8, :] + 0.125 * seen[j] for j in range(5)
        )
        for j in range(5):
            fresh[x, 0, 8 * j : 8 * j + 8, :] = total[j]
        write[x, 0, 2].start()
        carry = (turn, lagged, total)

        def harmonic(k, carry):
            now, late, total = carry
            keep = k <= count8
            c, s = jnp.where(keep, late[0], 0.0), jnp.where(keep, late[1], 0.0)
            wc, ws = 0.25 * now[0], 0.25 * now[1]
            sums = []
            for j in range(5):
                rows = slice(8 * j, 8 * j + 8)
                new_c = 0.875 * store[x, k, rows, :] + wc * seen[j]
                new_s = 0.875 * store[x, HARM + k, rows, :] + ws * seen[j]
                fresh[x, k, rows, :] = new_c
                fresh[x, HARM + k, rows, :] = new_s
                sums.append(total[j] + (new_c * c + new_s * s))
            return times_turn(now, turn), times_turn(late, lagged), tuple(sums)

        for g in range(GROUPS):
            for half in range(2):
                fetch[x, g, half].wait()
            carry = lax.fori_loop(1 + per * g, 1 + per * (g + 1), harmonic, carry)
            for half in range(2):
                write[x, g, half].start()
        for j in range(5):
            ghosts_out[x, 8 * j : 8 * j + 8, :] = carry[2][j]
    for copy in write.values():
        copy.wait()
    state_copy.wait()


def shards(flow_state, prior_state, fourier_store, sample_times, harmonics):
    cells = flow_state.shape
    store_flat = fourier_store.reshape(2, COEFS, 40, 128)
    anywhere = pl.BlockSpec(memory_space=pl.ANY)
    vmem = pl.BlockSpec(memory_space=pltpu.VMEM)
    state, samples = pl.pallas_call(
        sections_kernel,
        out_shape=(
            jax.ShapeDtypeStruct(cells, F32),
            jax.ShapeDtypeStruct((2, 40, 128), F32),
        ),
        in_specs=[anywhere] * 5,
        out_specs=(vmem, vmem),
        scratch_shapes=[
            pltpu.VMEM((5, 12, 32, 128), F32),
            pltpu.VMEM((5, 12, 32, 128), F32),
            pltpu.VMEM((5, 12, 32, 128), F32),
            pltpu.VMEM((5, 8, 32, 128), F32),
            pltpu.VMEM((2, COEFS, 40, 128), F32),
            pltpu.VMEM((2, 4, 128), jnp.int32),
            pltpu.VMEM((4, 128), jnp.int32),
            pltpu.VMEM((2, 40, 128), F32),
            pltpu.VMEM((6, 40, 128), F32),
            pltpu.VMEM((3, 2, 2, 5, 8, 128), F32),
            pltpu.VMEM((3, 2, 2, 5, 8, 128), F32),
            pltpu.VMEM((4, 40, 128), F32),
            pltpu.VMEM((2, 40, 128), F32),
            pltpu.SemaphoreType.DMA((6,)),
            pltpu.SemaphoreType.DMA((48,)),
            pltpu.SemaphoreType.DMA((48,)),
            pltpu.SemaphoreType.REGULAR((2,)),
        ],
        compiler_params=pltpu.CompilerParams(
            collective_id=0, has_side_effects=True, vmem_limit_bytes=24 * 1024 * 1024
        ),
        name="sections",
    )(flow_state, prior_state, store_flat, sample_times, harmonics)
    new_store, ghosts, new_state = pl.pallas_call(
        store_kernel,
        out_shape=(
            jax.ShapeDtypeStruct(store_flat.shape, F32),
            jax.ShapeDtypeStruct((2, 40, 128), F32),
            jax.ShapeDtypeStruct(cells, F32),
        ),
        in_specs=[anywhere, vmem, vmem, vmem, vmem],
        out_specs=(anywhere, vmem, anywhere),
        scratch_shapes=[
            pltpu.VMEM((2, COEFS, 40, 128), F32),
            pltpu.VMEM((2, COEFS, 40, 128), F32),
            pltpu.SemaphoreType.DMA((4 * GROUPS + 2,)),
            pltpu.SemaphoreType.DMA((4 * GROUPS + 3,)),
        ],
        compiler_params=pltpu.CompilerParams(vmem_limit_bytes=24 * 1024 * 1024),
        name="store",
    )(store_flat, sample_times, harmonics, samples, state)
    return (
        new_state,
        new_store.reshape(fourier_store.shape),
        ghosts.reshape(2, 10, 4, 128),
    )


def solution(mesh):
    placed = (
        P(None, "pitch", "blk", None),
        P(None, "pitch", "blk", None),
        P(None, None, None, ("blk", "pitch"), None),
        P(None, ("blk", "pitch"), None),
        P(("blk", "pitch"), None),
    )
    return jax.shard_map(
        shards,
        mesh=mesh,
        in_specs=placed,
        out_specs=(
            P(None, "pitch", "blk", None),
            P(None, None, None, ("blk", "pitch"), None),
            P(None, None, ("blk", "pitch"), None),
        ),
        check_vma=False,
    )
```

```python
import functools
import math

import jax
import jax.numpy as jnp
from jax import lax
from jax.experimental import pallas as pl
from jax.experimental.pallas import tpu as pltpu
from jax.sharding import PartitionSpec as P

MESH = pl.DeviceIdType.MESH
F32 = jnp.float32
NT = 96
HARM = 24
COEFS = 2 * HARM + 1
PERIOD = 2.0 * math.pi / NT
LAG = 2.0 * math.pi * 0.3
SECTIONS = (1.0 / 3.0, 0.5, 1.0)
CENTER = (8, 16)
EXTENDED = (4, 12, 20)


def twice(ref):
    rows = ref[...]
    return jnp.concatenate([rows, rows], axis=0)


def base_turn(times):
    quarter = (times - NT // 2).astype(F32) * (PERIOD / 4.0)
    sq = quarter * quarter
    s = quarter * (1.0 + sq * (-1.0 / 6 + sq * (1.0 / 120 + sq * (-1.0 / 5040 + sq * (1.0 / 362880)))))
    c = 1.0 + sq * (
        -0.5 + sq * (1.0 / 24 + sq * (-1.0 / 720 + sq * (1.0 / 40320 + sq * (-1.0 / 3628800))))
    )
    for _ in range(2):
        c, s = 1.0 - 2.0 * s * s, 2.0 * s * c
    return -c, -s


def turned(turn, angle):
    c, s = turn
    ca, sa = math.cos(angle), math.sin(angle)
    return c * ca - s * sa, s * ca + c * sa


def times_turn(a, b):
    return a[0] * b[0] - a[1] * b[1], a[1] * b[0] + a[0] * b[1]


def half_flux(cell, direction):
    rho, mp, ma, mr, energy = cell
    half_inv = 0.5 / rho
    kinetic = (mp * mp + ma * ma + mr * mr) * half_inv
    half_p = 0.2 * (energy - kinetic)
    moment = cell[direction]
    half_u = moment * half_inv
    parts = [
        0.5 * moment,
        mp * half_u,
        ma * half_u,
        mr * half_u,
        (energy + (half_p + half_p)) * half_u,
    ]
    parts[direction] = parts[direction] + half_p
    return parts


def section(s, cur, flow, prior, out, out_offsets, first, count, rows):
    step = 0.1 * SECTIONS[s]
    lane = lax.broadcasted_iota(jnp.int32, (8, 128), 1)
    at_low, at_high = lane == 0, lane == 127

    def after(x):
        return jnp.where(at_high, x, pltpu.roll(x, 127, 1))

    def before(x):
        return jnp.where(at_low, x, pltpu.roll(x, 1, 1))

    def layer(i, carry):
        at = first + i
        li = at + 2
        for r0 in rows:

            def load(dl, dr):
                return [cur[v, li + dl, r0 + dr : r0 + dr + 8, :] for v in range(5)]

            mid = load(0, 0)
            near = [load(1, 0), load(-1, 0), load(0, 1), load(0, -1)]
            far = [load(2, 0), load(-2, 0), load(0, 2), load(0, -2)]
            fluxes = [half_flux(near[k], 1 + k // 2) for k in range(4)]
            radial = half_flux(mid, 3)
            for v in range(5):
                total = (fluxes[0][v] - fluxes[1][v]) + (fluxes[2][v] - fluxes[3][v])
                n1 = (near[0][v] + near[1][v]) + (near[2][v] + near[3][v])
                n2 = (far[0][v] + far[1][v]) + (far[2][v] + far[3][v])
                x = mid[v]
                eighth = 0.125 * x
                up = (eighth + radial[v]) - 0.03125 * after(x)
                down = (eighth - radial[v]) - 0.03125 * before(x)
                total = total + (after(up) + before(down)) + (0.125 * n1 - 0.03125 * n2)
                base = (1.0 + 8.0 * step) * flow[v, li, r0 : r0 + 8, :] - (
                    2.0 * step
                ) * prior[v, at, r0 : r0 + 8, :]
                new = base - (6.0 - 0.5625) * step * x - step * total
                out[v, at + out_offsets[0], r0 + out_offsets[1] : r0 + out_offsets[1] + 8, :] = new
        return carry

    lax.fori_loop(0, count, layer, 0)


def sections_kernel(
    flow_hbm, prior_hbm, store_hbm, times_hbm, harm_hbm,
    state_out, samples_out,
    u0, u1, u2, prior, store, times, harm, share, ghosts,
    pack, land, faces, samples,
    local_sem, send_sem, recv_sem, ready_sem,
):
    p = lax.axis_index("pitch")
    b = lax.axis_index("blk")
    n_blk = lax.axis_size("blk")
    n_pitch = lax.axis_size("pitch")
    first_p, last_p = p == 0, p == n_pitch - 1
    is_end = jnp.logical_or(first_p, last_p)
    b_low, b_high = b > 0, b < n_blk - 1
    pitch_up = {"pitch": lax.rem(p + 1, n_pitch)}
    pitch_down = {"pitch": lax.rem(p + n_pitch - 1, n_pitch)}
    states = (u0, u1, u2)

    barrier = pltpu.get_barrier_semaphore()
    for where in (pitch_up, pitch_down):
        pl.semaphore_signal(barrier, inc=1, device_id=where, device_id_type=MESH)
    for where, cond in (({"blk": b - 1}, b_low), ({"blk": b + 1}, b_high)):

        @pl.when(cond)
        def _():
            pl.semaphore_signal(barrier, inc=1, device_id=where, device_id_type=MESH)

    loads = [
        pltpu.make_async_copy(flow_hbm, u0.at[:, 2:10, 8:24, :], local_sem.at[0]),
        pltpu.make_async_copy(store_hbm.at[0], store.at[0], local_sem.at[1]),
        pltpu.make_async_copy(store_hbm.at[1], store.at[1], local_sem.at[2]),
        pltpu.make_async_copy(prior_hbm, prior.at[:, :, 8:24, :], local_sem.at[3]),
        pltpu.make_async_copy(times_hbm, times, local_sem.at[4]),
        pltpu.make_async_copy(harm_hbm, harm, local_sem.at[5]),
    ]
    for k in (0, 4, 5, 1, 2, 3):
        loads[k].start()

    pl.semaphore_wait(barrier, 2 + b_low.astype(jnp.int32) + b_high.astype(jnp.int32))

    sent = []
    counter = [0]

    def remote(src, dst, where, send_if, recv_if):
        k = counter[0]
        counter[0] += 1
        copy = pltpu.make_async_remote_copy(
            src_ref=src,
            dst_ref=dst,
            send_sem=send_sem.at[k],
            recv_sem=recv_sem.at[k],
            device_id=where,
            device_id_type=MESH,
        )
        return copy, send_if, recv_if

    def send(*copies):
        for copy, send_if, _ in copies:
            sent.append((copy, send_if))

            @pl.when(send_if)
            def _():
                copy.start()

    def arrive(*copies):
        for copy, _, recv_if in copies:

            @pl.when(recv_if)
            def _():
                copy.wait_recv()

    not_first, not_last = p > 0, p < n_pitch - 1

    def pitch_pair(src, offset, target):
        return (
            remote(
                src.at[:, offset + 6 : offset + 8, 8 * (offset // 2) : 8 * (offset // 2) + 16, :],
                target.at[:, 0:2, 8:24, :], pitch_up, not_last, not_first,
            ),
            remote(
                src.at[:, offset : offset + 2, 8 * (offset // 2) : 8 * (offset // 2) + 16, :],
                target.at[:, 10:12, 8:24, :], pitch_down, not_first, not_last,
            ),
        )

    pitch = [pitch_pair(flow_hbm, 0, u0), pitch_pair(u1, 2, u1), pitch_pair(u2, 2, u2)]
    send(*pitch[0])

    g4 = jnp.where(first_p, 0, 4)
    up_ok, down_ok = jnp.logical_and(is_end, b_high), jnp.logical_and(is_end, b_low)
    wide = [
        remote(
            flow_hbm.at[:, pl.ds(g4, 4), 8:16, :], u0.at[:, pl.ds(2 + g4, 4), 0:8, :],
            {"blk": b + 1}, up_ok, down_ok,
        ),
        remote(
            flow_hbm.at[:, pl.ds(g4, 4), 0:8, :], u0.at[:, pl.ds(2 + g4, 4), 24:32, :],
            {"blk": b - 1}, down_ok, up_ok,
        ),
        remote(
            prior_hbm.at[:, pl.ds(g4, 4), 8:16, :], prior.at[:, pl.ds(g4, 4), 0:8, :],
            {"blk": b + 1}, up_ok, down_ok,
        ),
        remote(
            prior_hbm.at[:, pl.ds(g4, 4), 0:8, :], prior.at[:, pl.ds(g4, 4), 24:32, :],
            {"blk": b - 1}, down_ok, up_ok,
        ),
    ]

    for k, where in enumerate((pitch_up, pitch_down)):
        pl.semaphore_signal(ready_sem.at[k], inc=1, device_id=where, device_id_type=MESH)

    parts = ((2, 3, 4, 5), (0, 1, 6, 7))
    axial = [
        [
            (
                remote(pack.at[s, part, 0], land.at[s, part, 0], {"blk": b + 1}, b_high, b_low),
                remote(pack.at[s, part, 1], land.at[s, part, 1], {"blk": b - 1}, b_low, b_high),
            )
            for part in range(2)
        ]
        for s in range(3)
    ]

    def axial_send(s, part):
        for side, row in ((0, 22), (1, 8)):
            for v in range(5):
                for k, at in enumerate(parts[part]):
                    pack[s, part, side, v, 2 * k : 2 * k + 2, :] = states[s][
                        v, 2 + at, row : row + 2, :
                    ]
        send(*axial[s][part])

    def axial_take(s, part):
        for side, row, cond in ((0, 6, b_low), (1, 24, b_high)):

            @pl.when(cond)
            def _():
                axial[s][part][side][0].wait_recv()
                for v in range(5):
                    for k, at in enumerate(parts[part]):
                        states[s][v, 2 + at, row : row + 2, :] = land[
                            s, part, side, v, 2 * k : 2 * k + 2, :
                        ]

    def fill_edges(s, first, count):
        ref = states[s]
        for cond, row, source in ((b == 0, 6, 8), (b == n_blk - 1, 24, 23)):

            @pl.when(cond)
            def _():
                def layer(i, carry):
                    for v in range(5):
                        edge = ref[v, 2 + first + i, source : source + 1, :]
                        ref[v, 2 + first + i, row : row + 2, :] = jnp.broadcast_to(edge, (2, 128))
                    return carry

                lax.fori_loop(0, count, layer, 0)

    loads[0].wait()
    axial_send(0, 0)
    axial_send(0, 1)
    send(*wide)

    for k in (4, 5):
        loads[k].wait()
    count8 = twice(harm)
    for x in range(2):
        loads[1 + x].wait()
        turn = turned(base_turn(twice(times.at[x])), LAG if x else -LAG)

        def harmonic(k, carry):
            now, total = carry
            keep = k <= count8
            c, s = jnp.where(keep, now[0], 0.0), jnp.where(keep, now[1], 0.0)
            total = tuple(
                total[j]
                + (
                    store[x, k, 8 * j : 8 * j + 8, :] * c
                    + store[x, HARM + k, 8 * j : 8 * j + 8, :] * s
                )
                for j in range(5)
            )
            return times_turn(now, turn), total

        start = tuple(store[x, 0, 8 * j : 8 * j + 8, :] for j in range(5))
        _, total = lax.fori_loop(1, HARM + 1, harmonic, (turn, start))
        for j in range(5):
            share[x, 8 * j : 8 * j + 8, :] = total[j]

    for k in range(2):
        pl.semaphore_wait(ready_sem.at[k], 1)

    ghost_copies = []
    for j in range(4):
        for x, target in ((0, 0), (1, 3)):
            if j != target:
                ghost_copies.append(
                    (
                        j,
                        x,
                        remote(
                            share.at[x], ghosts.at[1 + j], {"pitch": target},
                            p == j, p == target,
                        ),
                    )
                )
    beside = []
    for x, target in ((0, 0), (1, 3)):
        beside.append(
            remote(
                share.at[x], ghosts.at[0], {"blk": b + 1, "pitch": target},
                jnp.logical_and(last_p, b_high), jnp.logical_and(p == target, b_low),
            )
        )
        beside.append(
            remote(
                share.at[x], ghosts.at[5], {"blk": b - 1, "pitch": target},
                jnp.logical_and(first_p, b_low), jnp.logical_and(p == target, b_high),
            )
        )
    ghost_copies = [c[2] for c in ghost_copies] + beside
    send(*ghost_copies)
    for x, cond, slot in ((0, first_p, 1), (1, last_p, 4)):

        @pl.when(cond)
        def _():
            ghosts[slot] = share[x]

    def inner(s):
        fill_edges(s, 0, 8)
        if s < 2:
            section(s, states[s], u0, prior, states[s + 1], (2, 0), 2, 4, CENTER)
        else:
            section(s, states[s], u0, prior, state_out, (0, -8), 2, 4, CENTER)

    def pair(s, first):
        if s < 2:
            section(s, states[s], u0, prior, states[s + 1], (2, 0), first, 2, CENTER)
        else:
            section(s, states[s], u0, prior, state_out, (0, -8), first, 2, CENTER)

    def outer(s):
        for side, cond, first in ((1, not_last, 6), (0, not_first, 0)):

            @pl.when(cond)
            def _():
                pitch[s][side][0].wait_recv()
                pair(s, first)
                if s < 2:
                    pitch[s + 1][1 - side][0].start()

        if s < 2:
            sent.extend((c[0], c[1]) for c in pitch[s + 1])

    loads[3].wait()
    arrive(*wide[:2])
    axial_take(0, 0)
    axial_take(0, 1)
    inner(0)
    axial_send(1, 0)
    outer(0)
    axial_send(1, 1)

    face_copies = []
    for x, source in ((0, 3), (1, 0)):
        for j in range(4):
            if j != source:
                face_copies.append(
                    remote(faces.at[j], samples.at[x], {"pitch": j}, p == source, p == j)
                )

    @pl.when(is_end)
    def _():
        arrive(*wide[2:])
        arrive(*ghost_copies)
        g2 = jnp.where(first_p, 0, 10)
        for k in range(6):

            @pl.when(jnp.logical_or(jnp.logical_and(k > 0, k < 5), b_low if k == 0 else b_high))
            def _():
                for v in range(5):
                    for layer in range(2):
                        at = (2 * v + layer) * 4
                        block = ghosts[k, at : at + 4, :]
                        for ref in states:
                            ref[v, g2 + layer, 4 + 4 * k : 8 + 4 * k, :] = block

        near = jnp.where(first_p, 0, 6)
        beyond = jnp.where(first_p, 2, 4)
        section(0, u0, u0, prior, u1, (2, 0), near, 2, EXTENDED)
        section(0, u0, u0, prior, u1, (2, 0), beyond, 2, EXTENDED)
        fill_edges(1, g4, 4)
        section(1, u1, u0, prior, u2, (2, 0), near, 2, EXTENDED)
        section(1, u1, u0, prior, u2, (2, 0), beyond, 2, CENTER)
        fill_edges(2, g4, 4)
        section(2, u2, u0, prior, state_out, (0, -8), near, 2, CENTER)
        for j in range(4):
            for v in range(5):
                for layer in range(2):
                    at = (2 * v + layer) * 4
                    faces[j, at : at + 4, :] = state_out[v, near + layer, 4 * j : 4 * j + 4, :]

    send(*face_copies)
    for x, cond, slot in ((1, first_p, 0), (0, last_p, 3)):

        @pl.when(cond)
        def _():
            samples[x] = faces[slot]

    for s in (1, 2):
        axial_take(s, 0)
        axial_take(s, 1)
        inner(s)
        if s == 1:
            axial_send(2, 0)
        outer(s)
        if s == 1:
            axial_send(2, 1)

    arrive(*face_copies)
    samples_out[...] = samples[...]
    for copy, cond in sent:

        @pl.when(cond)
        def _():
            copy.wait_send()


GROUPS = 4


def store_kernel(
    store, times_ref, harm_ref, samples, state, store_out, ghosts_out, state_out, fresh, out_sem
):
    per = HARM // GROUPS
    state_copy = pltpu.make_async_copy(state, state_out, out_sem.at[0])
    state_copy.start()
    writes = [state_copy]

    def write(x, first, count):
        rows = pl.ds(first, count)
        copy = pltpu.make_async_copy(
            fresh.at[x, rows], store_out.at[x, rows], out_sem.at[len(writes)]
        )
        copy.start()
        writes.append(copy)

    count8 = twice(harm_ref)
    for x in range(2):
        turn = turned(base_turn(twice(times_ref.at[x])), PERIOD)
        lagged = turned(turn, LAG if x else -LAG)
        seen = tuple(samples[x, 8 * j : 8 * j + 8, :] for j in range(5))
        total = tuple(
            0.875 * store[x, 0, 8 * j : 8 * j + 8, :] + 0.125 * seen[j] for j in range(5)
        )
        for j in range(5):
            fresh[x, 0, 8 * j : 8 * j + 8, :] = total[j]
        write(x, 0, 1)
        carry = (turn, lagged, total)

        def harmonic(k, carry):
            now, late, total = carry
            keep = k <= count8
            c, s = jnp.where(keep, late[0], 0.0), jnp.where(keep, late[1], 0.0)
            wc, ws = 0.25 * now[0], 0.25 * now[1]
            sums = []
            for j in range(5):
                rows = slice(8 * j, 8 * j + 8)
                new_c = 0.875 * store[x, k, rows, :] + wc * seen[j]
                new_s = 0.875 * store[x, HARM + k, rows, :] + ws * seen[j]
                fresh[x, k, rows, :] = new_c
                fresh[x, HARM + k, rows, :] = new_s
                sums.append(total[j] + (new_c * c + new_s * s))
            return times_turn(now, turn), times_turn(late, lagged), tuple(sums)

        for g in range(GROUPS):
            carry = lax.fori_loop(1 + per * g, 1 + per * (g + 1), harmonic, carry, unroll=2)
            for half in range(2):
                write(x, 1 + HARM * half + per * g, per)
        for j in range(5):
            ghosts_out[x, 8 * j : 8 * j + 8, :] = carry[2][j]
    for copy in writes:
        copy.wait()


def shards(flow_state, prior_state, fourier_store, sample_times, harmonics):
    cells = flow_state.shape
    store_flat = fourier_store.reshape(2, COEFS, 40, 128)
    anywhere = pl.BlockSpec(memory_space=pl.ANY)
    vmem = pl.BlockSpec(memory_space=pltpu.VMEM)
    state, samples = pl.pallas_call(
        sections_kernel,
        out_shape=(
            jax.ShapeDtypeStruct(cells, F32),
            jax.ShapeDtypeStruct((2, 40, 128), F32),
        ),
        in_specs=[pl.BlockSpec(memory_space=pltpu.HBM)] * 5,
        out_specs=(vmem, vmem),
        scratch_shapes=[
            pltpu.VMEM((5, 12, 32, 128), F32),
            pltpu.VMEM((5, 12, 32, 128), F32),
            pltpu.VMEM((5, 12, 32, 128), F32),
            pltpu.VMEM((5, 8, 32, 128), F32),
            pltpu.VMEM((2, COEFS, 40, 128), F32),
            pltpu.VMEM((2, 4, 128), jnp.int32),
            pltpu.VMEM((4, 128), jnp.int32),
            pltpu.VMEM((2, 40, 128), F32),
            pltpu.VMEM((6, 40, 128), F32),
            pltpu.VMEM((3, 2, 2, 5, 8, 128), F32),
            pltpu.VMEM((3, 2, 2, 5, 8, 128), F32),
            pltpu.VMEM((4, 40, 128), F32),
            pltpu.VMEM((2, 40, 128), F32),
            pltpu.SemaphoreType.DMA((6,)),
            pltpu.SemaphoreType.DMA((48,)),
            pltpu.SemaphoreType.DMA((48,)),
            pltpu.SemaphoreType.REGULAR((2,)),
        ],
        compiler_params=pltpu.CompilerParams(
            collective_id=0, has_side_effects=True, vmem_limit_bytes=24 * 1024 * 1024
        ),
        name="sections",
    )(*[pltpu.with_memory_space_constraint(x, pltpu.HBM) for x in (flow_state, prior_state, store_flat, sample_times, harmonics)])
    new_store, ghosts, new_state = pl.pallas_call(
        store_kernel,
        out_shape=(
            jax.ShapeDtypeStruct(store_flat.shape, F32),
            jax.ShapeDtypeStruct((2, 40, 128), F32),
            jax.ShapeDtypeStruct(cells, F32),
        ),
        in_specs=[vmem, vmem, vmem, vmem, anywhere],
        out_specs=(anywhere, vmem, anywhere),
        scratch_shapes=[
            pltpu.VMEM((2, COEFS, 40, 128), F32),
            pltpu.SemaphoreType.DMA((4 * GROUPS + 3,)),
        ],
        compiler_params=pltpu.CompilerParams(vmem_limit_bytes=24 * 1024 * 1024),
        name="store",
    )(store_flat, sample_times, harmonics, samples, state)
    return (
        new_state,
        new_store.reshape(fourier_store.shape),
        ghosts.reshape(2, 10, 4, 128),
    )


def solution(mesh):
    placed = (
        P(None, "pitch", "blk", None),
        P(None, "pitch", "blk", None),
        P(None, None, None, ("blk", "pitch"), None),
        P(None, ("blk", "pitch"), None),
        P(("blk", "pitch"), None),
    )
    return jax.shard_map(
        shards,
        mesh=mesh,
        in_specs=placed,
        out_specs=(
            P(None, "pitch", "blk", None),
            P(None, None, None, ("blk", "pitch"), None),
            P(None, None, ("blk", "pitch"), None),
        ),
        check_vma=False,
    )
```

```python
import functools
import math

import jax
import jax.numpy as jnp
from jax import lax
from jax.experimental import pallas as pl
from jax.experimental.pallas import tpu as pltpu
from jax.sharding import PartitionSpec as P

MESH = pl.DeviceIdType.MESH
F32 = jnp.float32
NT = 96
HARM = 24
COEFS = 2 * HARM + 1
PERIOD = 2.0 * math.pi / NT
LAG = 2.0 * math.pi * 0.3
SECTIONS = (1.0 / 3.0, 0.5, 1.0)
CENTER = (8, 16)
EXTENDED = (4, 12, 20)


def twice(ref):
    rows = ref[...]
    return jnp.concatenate([rows, rows], axis=0)


def base_turn(times):
    quarter = (times - NT // 2).astype(F32) * (PERIOD / 4.0)
    sq = quarter * quarter
    s = quarter * (1.0 + sq * (-1.0 / 6 + sq * (1.0 / 120 + sq * (-1.0 / 5040 + sq * (1.0 / 362880)))))
    c = 1.0 + sq * (
        -0.5 + sq * (1.0 / 24 + sq * (-1.0 / 720 + sq * (1.0 / 40320 + sq * (-1.0 / 3628800))))
    )
    for _ in range(2):
        c, s = 1.0 - 2.0 * s * s, 2.0 * s * c
    return -c, -s


def turned(turn, angle):
    c, s = turn
    ca, sa = math.cos(angle), math.sin(angle)
    return c * ca - s * sa, s * ca + c * sa


def times_turn(a, b):
    return a[0] * b[0] - a[1] * b[1], a[1] * b[0] + a[0] * b[1]


def half_flux(cell, direction):
    rho, mp, ma, mr, energy = cell
    inv = pl.reciprocal(rho, approx=True)
    half_inv = inv * (1.0 - (0.5 * rho) * inv)
    kinetic = (mp * mp + ma * ma + mr * mr) * half_inv
    half_p = 0.2 * (energy - kinetic)
    moment = cell[direction]
    half_u = moment * half_inv
    parts = [
        0.5 * moment,
        mp * half_u,
        ma * half_u,
        mr * half_u,
        (energy + (half_p + half_p)) * half_u,
    ]
    parts[direction] = parts[direction] + half_p
    return parts


def section(s, cur, flow, prior, out, out_offsets, first, count, rows):
    step = 0.1 * SECTIONS[s]
    lane = lax.broadcasted_iota(jnp.int32, (8, 128), 1)
    at_low, at_high = lane == 0, lane == 127

    def after(x):
        return jnp.where(at_high, x, pltpu.roll(x, 127, 1))

    def before(x):
        return jnp.where(at_low, x, pltpu.roll(x, 1, 1))

    def layer(i, carry):
        at = first + i
        li = at + 2
        for r0 in rows:

            def load(dl, dr):
                return [cur[v, li + dl, pl.ds(r0 + dr, 8), :] for v in range(5)]

            mid = load(0, 0)
            near = [load(1, 0), load(-1, 0), load(0, 1), load(0, -1)]
            far = [load(2, 0), load(-2, 0), load(0, 2), load(0, -2)]
            fluxes = [half_flux(near[k], 1 + k // 2) for k in range(4)]
            radial = half_flux(mid, 3)
            for v in range(5):
                total = (fluxes[0][v] - fluxes[1][v]) + (fluxes[2][v] - fluxes[3][v])
                n1 = (near[0][v] + near[1][v]) + (near[2][v] + near[3][v])
                n2 = (far[0][v] + far[1][v]) + (far[2][v] + far[3][v])
                x = mid[v]
                eighth = 0.125 * x
                up = (eighth + radial[v]) - 0.03125 * after(x)
                down = (eighth - radial[v]) - 0.03125 * before(x)
                total = total + (after(up) + before(down)) + (0.125 * n1 - 0.03125 * n2)
                base = (1.0 + 8.0 * step) * flow[v, li, pl.ds(r0, 8), :] - (
                    2.0 * step
                ) * prior[v, at, pl.ds(r0, 8), :]
                new = base - (6.0 - 0.5625) * step * x - step * total
                out[v, at + out_offsets[0], pl.ds(r0 + out_offsets[1], 8), :] = new
        return carry

    lax.fori_loop(0, count, layer, 0)


def sections_kernel(
    flow_hbm, prior_hbm, store_hbm, times_hbm, harm_hbm,
    state_out, samples_out,
    u0, u1, u2, prior, store, times, harm, share, ghosts, relay, faces, samples,
    local_sem, send_sem, recv_sem, word_sem,
):
    p = lax.axis_index("pitch")
    b = lax.axis_index("blk")
    n_blk = lax.axis_size("blk")
    last = lax.axis_size("pitch") - 1
    first_p, last_p = p == 0, p == last
    not_first, not_last = p > 0, p < last
    is_end = jnp.logical_or(first_p, last_p)
    b_low, b_high = b > 0, b < n_blk - 1
    above, below = {"pitch": p + 1}, {"pitch": p - 1}
    states = (u0, u1, u2)
    both = jnp.logical_and

    def signal(sem, where, cond):
        @pl.when(cond)
        def _():
            pl.semaphore_signal(sem, inc=1, device_id=where, device_id_type=MESH)

    def await_word(k, cond):
        @pl.when(cond)
        def _():
            pl.semaphore_wait(word_sem.at[k], 1)

    def number(cond):
        return cond.astype(jnp.int32)

    barrier = pltpu.get_barrier_semaphore()
    signal(barrier, above, not_last)
    signal(barrier, {"blk": b - 1}, b_low)
    signal(barrier, {"blk": b + 1}, b_high)
    signal(barrier, {"pitch": last}, first_p)
    signal(barrier, {"blk": b - 1, "pitch": last}, both(first_p, b_low))

    loads = [
        pltpu.make_async_copy(flow_hbm, u0.at[:, 2:10, 8:24, :], local_sem.at[0]),
        pltpu.make_async_copy(store_hbm.at[0], store.at[0], local_sem.at[1]),
        pltpu.make_async_copy(store_hbm.at[1], store.at[1], local_sem.at[2]),
        pltpu.make_async_copy(prior_hbm, prior.at[:, :, 8:24, :], local_sem.at[3]),
        pltpu.make_async_copy(times_hbm, times, local_sem.at[4]),
        pltpu.make_async_copy(harm_hbm, harm, local_sem.at[5]),
    ]
    for k in (0, 4, 5, 1, 2, 3):
        loads[k].start()

    pl.semaphore_wait(
        barrier,
        number(not_first) + number(b_low) + number(b_high)
        + number(last_p) * (1 + number(b_high)),
    )
    signal(word_sem.at[0], below, not_first)
    signal(word_sem.at[1], {"pitch": 0}, last_p)

    sent = []

    def remote(src, dst, where, send_if, recv_if):
        k = len(sent)
        copy = pltpu.make_async_remote_copy(
            src_ref=src,
            dst_ref=dst,
            send_sem=send_sem.at[k],
            recv_sem=recv_sem.at[k],
            device_id=where,
            device_id_type=MESH,
        )
        sent.append((copy, send_if))
        return copy, send_if, recv_if

    def send(*copies):
        for copy, send_if, _ in copies:

            @pl.when(send_if)
            def _():
                copy.start()

    def arrive(*copies):
        for copy, _, recv_if in copies:

            @pl.when(recv_if)
            def _():
                copy.wait_recv()

    chunk_low = [lax.rem(b + t, 2) == 0 for t in range(2)]
    chunk_row = [pl.multiple_of(jnp.where(low, 8, 16), 8) for low in chunk_low]

    def pitch_copies(src, layer, shift, target):
        made = []
        for row in chunk_row:
            rows, there = pl.ds(pl.multiple_of(row - shift, 8), 8), pl.ds(row, 8)
            made.append(
                (
                    remote(
                        src.at[:, layer + 6 : layer + 8, rows, :], target.at[:, 0:2, there, :],
                        above, not_last, not_first,
                    ),
                    remote(
                        src.at[:, layer : layer + 2, rows, :], target.at[:, 10:12, there, :],
                        below, not_first, not_last,
                    ),
                )
            )
        return made

    pitch = [pitch_copies(flow_hbm, 0, 8, u0), pitch_copies(u1, 2, 0, u1), pitch_copies(u2, 2, 0, u2)]
    send(pitch[0][0][1], pitch[0][1][1])

    g6 = jnp.where(first_p, 0, 2)
    g4 = jnp.where(first_p, 0, 4)

    def beside(src, source, target, layers, count, shift, rows, cond, skip=0):
        there = pl.ds(layers + shift, count)
        here = pl.ds(layers + source[2], count)
        low, high = source[0], source[1]
        return (
            remote(
                src.at[:, here, high - skip - rows : high - skip, :],
                target.at[:, there, 8 - skip - rows : 8 - skip, :],
                {"blk": b + 1}, both(cond, b_high), both(cond, b_low),
            ),
            remote(
                src.at[:, here, low + skip : low + skip + rows, :],
                target.at[:, there, 24 + skip : 24 + skip + rows, :],
                {"blk": b - 1}, both(cond, b_low), both(cond, b_high),
            ),
        )

    plain, padded = (0, 16, 0), (8, 24, 2)
    flow_sides = beside(flow_hbm, plain, u0, 0, 8, 2, 2, p >= 0)
    flow_more = beside(flow_hbm, plain, u0, g6, 6, 2, 4, is_end, 2)
    prior_sides = beside(prior_hbm, plain, prior, g4, 4, 0, 4, is_end)
    send(*flow_sides)

    def exchanged(s, q):
        ends = [0] if s == 1 else [0, 1]
        skip_first = both(first_p, jnp.asarray(q in ends))
        skip_last = both(last_p, jnp.asarray(3 - q in ends))
        return jnp.logical_not(jnp.logical_or(skip_first, skip_last))

    axial = {
        (s, q): beside(states[s], padded, states[s], 2 * q, 2, 2, 2, exchanged(s, q))
        for s in (1, 2)
        for q in range(4)
    }

    def outer_sides(s, t, wait):
        for q in (0, 3):
            to_above, to_below = axial[s, q]
            for low in (True, False):
                copy, send_if, recv_if = to_below if low != wait else to_above
                cond = both(recv_if if wait else send_if, chunk_low[t] == low)

                @pl.when(cond)
                def _():
                    copy.wait_recv() if wait else copy.start()

    for k in (4, 5):
        loads[k].wait()
    count8 = twice(harm)
    for x in range(2):
        loads[1 + x].wait()
        turn = turned(base_turn(twice(times.at[x])), LAG if x else -LAG)

        def harmonic(k, carry):
            now, total = carry
            keep = k <= count8
            c, s = jnp.where(keep, now[0], 0.0), jnp.where(keep, now[1], 0.0)
            total = tuple(
                total[j]
                + (
                    store[x, k, 8 * j : 8 * j + 8, :] * c
                    + store[x, HARM + k, 8 * j : 8 * j + 8, :] * s
                )
                for j in range(5)
            )
            return times_turn(now, turn), total

        start = tuple(store[x, 0, 8 * j : 8 * j + 8, :] for j in range(5))
        _, total = lax.fori_loop(1, HARM + 1, harmonic, (turn, start))
        for j in range(5):
            share[x, 8 * j : 8 * j + 8, :] = total[j]

    low_early = [
        remote(share.at[0], ghosts.at[2], {"pitch": 0}, p == 1, first_p),
        remote(share.at[0], ghosts.at[4], {"pitch": 0}, last_p, first_p),
        remote(
            share.at[0], ghosts.at[0], {"blk": b + 1, "pitch": 0},
            both(last_p, b_high), both(first_p, b_low),
        ),
        remote(
            share.at[0], ghosts.at[5], {"blk": b - 1, "pitch": 0},
            both(first_p, b_low), both(first_p, b_high),
        ),
    ]
    low_later = remote(share.at[0], ghosts.at[3], {"pitch": 0}, p == 2, first_p)
    relayed = remote(share.at[1], relay.at[1], {"pitch": 0}, p == 1, first_p)
    high_early = remote(
        share.at[1], ghosts.at[0], {"blk": b + 1, "pitch": last},
        both(last_p, b_high), both(last_p, b_low),
    )
    high_next = remote(share.at[1], ghosts.at[3], {"pitch": last}, p == 2, last_p)
    high_relay = remote(relay, ghosts.at[1:3], {"pitch": last}, first_p, last_p)
    high_beside = remote(
        share.at[1], ghosts.at[5], {"blk": b - 1, "pitch": last},
        both(first_p, b_low), both(last_p, b_high),
    )
    send(*low_early, relayed, high_early, *flow_more, *prior_sides)

    await_word(0, not_last)
    send(pitch[0][0][0], pitch[0][1][0])
    signal(word_sem.at[2], above, jnp.logical_or(p == 1, p == 2))
    send(high_next)
    await_word(2, p == 2)
    send(low_later)

    def fill_edges(s, first, count):
        ref = states[s]
        for cond, row, source in ((b == 0, 6, 8), (b == n_blk - 1, 24, 23)):

            @pl.when(cond)
            def _():
                def layer(i, carry):
                    for v in range(5):
                        edge = ref[v, 2 + first + i, source : source + 1, :]
                        ref[v, 2 + first + i, row : row + 2, :] = jnp.broadcast_to(edge, (2, 128))
                    return carry

                lax.fori_loop(0, count, layer, 0)

    def update(s, first, count, rows):
        if s < 2:
            section(s, states[s], u0, prior, states[s + 1], (2, 0), first, count, rows)
        else:
            section(s, states[s], u0, prior, state_out, (0, -8), first, count, rows)

    def all_layers(s, between=None):
        fill_edges(s, 0, 8)
        for t in range(2):
            if s > 0:
                outer_sides(s, t, True)
            for side, cond, first in ((0, not_first, 0), (1, not_last, 6)):

                @pl.when(cond)
                def _():
                    pitch[s][t][side][0].wait_recv()
                    update(s, first, 2, (chunk_row[t],))
                    if s < 2:
                        pitch[s + 1][t][1 - side][0].start()

            if s < 2:
                outer_sides(s + 1, t, False)
            if t == 0:
                if s > 0:
                    arrive(*axial[s, 1], *axial[s, 2])
                if s == 1:
                    m2 = jnp.where(first_p, 4, 2)
                    update(s, jnp.where(is_end, m2, 2), jnp.where(is_end, 2, 4), CENTER)
                else:
                    update(s, 2, 4, CENTER)
                if s < 2:
                    send(*axial[s + 1, 1], *axial[s + 1, 2])
                if between:
                    between()

    loads[0].wait()
    loads[3].wait()
    arrive(*flow_sides)
    all_layers(0)

    @pl.when(first_p)
    def _():
        pl.semaphore_wait(word_sem.at[1], 1)
        relay[0] = share[1]
        relayed[0].wait_recv()
        high_relay[0].start()

    send(high_beside)
    face_copies = []
    for x, source in ((0, 3), (1, 0)):
        for j in range(4):
            if j != source:
                face_copies.append(
                    remote(faces.at[j], samples.at[x], {"pitch": j}, p == source, p == j)
                )

    def ghosts_chain():
        @pl.when(is_end)
        def _():
            arrive(*flow_more, *prior_sides, *low_early, low_later, high_early, high_next, high_relay, high_beside)
            pl.when(first_p)(lambda: ghosts.__setitem__(1, share[0]))
            pl.when(last_p)(lambda: ghosts.__setitem__(4, share[1]))
            outside = jnp.where(first_p, 0, 10)
            for k in range(6):

                @pl.when(b_low if k == 0 else (b_high if k == 5 else is_end))
                def _():
                    for v in range(5):
                        for layer in range(2):
                            at = (2 * v + layer) * 4
                            block = ghosts[k, at : at + 4, :]
                            for ref in states:
                                ref[v, outside + layer, 4 + 4 * k : 8 + 4 * k, :] = block

            for q, mine in ((1, first_p), (2, last_p)):
                for copy, send_if, _ in axial[1, q]:

                    @pl.when(both(send_if, mine))
                    def _():
                        copy.wait_send()

            near = jnp.where(first_p, 0, 6)
            update(0, g4, 4, EXTENDED)
            fill_edges(1, g4, 4)
            update(1, g4, 4, EXTENDED)
            fill_edges(2, g4, 4)
            update(2, near, 2, CENTER)
            for j in range(4):
                for v in range(5):
                    for layer in range(2):
                        at = (2 * v + layer) * 4
                        faces[j, at : at + 4, :] = state_out[v, near + layer, 4 * j : 4 * j + 4, :]

        await_word(2, last_p)
        send(*face_copies)
        pl.when(first_p)(lambda: samples.__setitem__(1, faces[0]))
        pl.when(last_p)(lambda: samples.__setitem__(0, faces[3]))

    all_layers(1, ghosts_chain)
    all_layers(2)
    arrive(*face_copies)
    samples_out[...] = samples[...]
    early = [(axial[1, 1], first_p), (axial[1, 2], last_p)]
    for copy, cond in sent:
        for copies, mine in early:
            if any(copy is made[0] for made in copies):
                cond = both(cond, jnp.logical_not(mine))

        @pl.when(cond)
        def _():
            copy.wait_send()


GROUPS = 4


def store_kernel(
    store, times_ref, harm_ref, samples, state, store_out, ghosts_out, state_out, fresh, out_sem
):
    per = HARM // GROUPS
    state_copy = pltpu.make_async_copy(state, state_out, out_sem.at[0])
    state_copy.start()
    writes = [state_copy]

    def write(x, first, count):
        rows = pl.ds(first, count)
        copy = pltpu.make_async_copy(
            fresh.at[x, rows], store_out.at[x, rows], out_sem.at[len(writes)]
        )
        copy.start()
        writes.append(copy)

    count8 = twice(harm_ref)
    for x in range(2):
        turn = turned(base_turn(twice(times_ref.at[x])), PERIOD)
        lagged = turned(turn, LAG if x else -LAG)
        seen = tuple(samples[x, 8 * j : 8 * j + 8, :] for j in range(5))
        total = tuple(
            0.875 * store[x, 0, 8 * j : 8 * j + 8, :] + 0.125 * seen[j] for j in range(5)
        )
        for j in range(5):
            fresh[x, 0, 8 * j : 8 * j + 8, :] = total[j]
        write(x, 0, 1)
        carry = (turn, lagged, total)

        def harmonic(k, carry):
            now, late, total = carry
            keep = k <= count8
            c, s = jnp.where(keep, late[0], 0.0), jnp.where(keep, late[1], 0.0)
            wc, ws = 0.25 * now[0], 0.25 * now[1]
            sums = []
            for j in range(5):
                rows = slice(8 * j, 8 * j + 8)
                new_c = 0.875 * store[x, k, rows, :] + wc * seen[j]
                new_s = 0.875 * store[x, HARM + k, rows, :] + ws * seen[j]
                fresh[x, k, rows, :] = new_c
                fresh[x, HARM + k, rows, :] = new_s
                sums.append(total[j] + (new_c * c + new_s * s))
            return times_turn(now, turn), times_turn(late, lagged), tuple(sums)

        for g in range(GROUPS):
            carry = lax.fori_loop(1 + per * g, 1 + per * (g + 1), harmonic, carry, unroll=2)
            for half in range(2):
                write(x, 1 + HARM * half + per * g, per)
        for j in range(5):
            ghosts_out[x, 8 * j : 8 * j + 8, :] = carry[2][j]
    for copy in writes:
        copy.wait()


def shards(flow_state, prior_state, fourier_store, sample_times, harmonics):
    cells = flow_state.shape
    store_flat = fourier_store.reshape(2, COEFS, 40, 128)
    anywhere = pl.BlockSpec(memory_space=pl.ANY)
    vmem = pl.BlockSpec(memory_space=pltpu.VMEM)
    state, samples = pl.pallas_call(
        sections_kernel,
        out_shape=(
            jax.ShapeDtypeStruct(cells, F32),
            jax.ShapeDtypeStruct((2, 40, 128), F32),
        ),
        in_specs=[pl.BlockSpec(memory_space=pltpu.HBM)] * 5,
        out_specs=(vmem, vmem),
        scratch_shapes=[
            pltpu.VMEM((5, 12, 32, 128), F32),
            pltpu.VMEM((5, 12, 32, 128), F32),
            pltpu.VMEM((5, 12, 32, 128), F32),
            pltpu.VMEM((5, 8, 32, 128), F32),
            pltpu.VMEM((2, COEFS, 40, 128), F32),
            pltpu.VMEM((2, 4, 128), jnp.int32),
            pltpu.VMEM((4, 128), jnp.int32),
            pltpu.VMEM((2, 40, 128), F32),
            pltpu.VMEM((6, 40, 128), F32),
            pltpu.VMEM((2, 40, 128), F32),
            pltpu.VMEM((4, 40, 128), F32),
            pltpu.VMEM((2, 40, 128), F32),
            pltpu.SemaphoreType.DMA((6,)),
            pltpu.SemaphoreType.DMA((64,)),
            pltpu.SemaphoreType.DMA((64,)),
            pltpu.SemaphoreType.REGULAR((3,)),
        ],
        compiler_params=pltpu.CompilerParams(
            collective_id=0, has_side_effects=True, vmem_limit_bytes=24 * 1024 * 1024
        ),
        name="sections",
    )(*[pltpu.with_memory_space_constraint(x, pltpu.HBM) for x in (flow_state, prior_state, store_flat, sample_times, harmonics)])
    new_store, ghosts, new_state = pl.pallas_call(
        store_kernel,
        out_shape=(
            jax.ShapeDtypeStruct(store_flat.shape, F32),
            jax.ShapeDtypeStruct((2, 40, 128), F32),
            jax.ShapeDtypeStruct(cells, F32),
        ),
        in_specs=[vmem, vmem, vmem, vmem, anywhere],
        out_specs=(anywhere, vmem, anywhere),
        scratch_shapes=[
            pltpu.VMEM((2, COEFS, 40, 128), F32),
            pltpu.SemaphoreType.DMA((4 * GROUPS + 3,)),
        ],
        compiler_params=pltpu.CompilerParams(vmem_limit_bytes=24 * 1024 * 1024),
        name="store",
    )(store_flat, sample_times, harmonics, samples, state)
    return (
        new_state,
        new_store.reshape(fourier_store.shape),
        ghosts.reshape(2, 10, 4, 128),
    )


def solution(mesh):
    placed = (
        P(None, "pitch", "blk", None),
        P(None, "pitch", "blk", None),
        P(None, None, None, ("blk", "pitch"), None),
        P(None, ("blk", "pitch"), None),
        P(("blk", "pitch"), None),
    )
    return jax.shard_map(
        shards,
        mesh=mesh,
        in_specs=placed,
        out_specs=(
            P(None, "pitch", "blk", None),
            P(None, None, None, ("blk", "pitch"), None),
            P(None, None, ("blk", "pitch"), None),
        ),
        check_vma=False,
    )
```

```python
import functools
import math

import jax
import jax.numpy as jnp
from jax import lax
from jax.experimental import pallas as pl
from jax.experimental.pallas import tpu as pltpu
from jax.sharding import PartitionSpec as P

MESH = pl.DeviceIdType.MESH
F32 = jnp.float32
NT = 96
HARM = 24
COEFS = 2 * HARM + 1
PERIOD = 2.0 * math.pi / NT
LAG = 2.0 * math.pi * 0.3
SECTIONS = (1.0 / 3.0, 0.5, 1.0)
CENTER = (8, 16)
EXTENDED = (4, 12, 20)


def twice(ref):
    rows = ref[...]
    return jnp.concatenate([rows, rows], axis=0)


def base_turn(times):
    quarter = (times - NT // 2).astype(F32) * (PERIOD / 4.0)
    sq = quarter * quarter
    s = quarter * (1.0 + sq * (-1.0 / 6 + sq * (1.0 / 120 + sq * (-1.0 / 5040 + sq * (1.0 / 362880)))))
    c = 1.0 + sq * (
        -0.5 + sq * (1.0 / 24 + sq * (-1.0 / 720 + sq * (1.0 / 40320 + sq * (-1.0 / 3628800))))
    )
    for _ in range(2):
        c, s = 1.0 - 2.0 * s * s, 2.0 * s * c
    return -c, -s


def turned(turn, angle):
    c, s = turn
    ca, sa = math.cos(angle), math.sin(angle)
    return c * ca - s * sa, s * ca + c * sa


def times_turn(a, b):
    return a[0] * b[0] - a[1] * b[1], a[1] * b[0] + a[0] * b[1]


def half_flux(cell, direction):
    rho, mp, ma, mr, energy = cell
    inv = pl.reciprocal(rho, approx=True)
    half_inv = inv * (1.0 - (0.5 * rho) * inv)
    kinetic = (mp * mp + ma * ma + mr * mr) * half_inv
    half_p = 0.2 * (energy - kinetic)
    moment = cell[direction]
    half_u = moment * half_inv
    parts = [
        0.5 * moment,
        mp * half_u,
        ma * half_u,
        mr * half_u,
        (energy + (half_p + half_p)) * half_u,
    ]
    parts[direction] = parts[direction] + half_p
    return parts


def section(s, cur, flow, prior, out, out_offsets, first, count, rows):
    step = 0.1 * SECTIONS[s]
    lane = lax.broadcasted_iota(jnp.int32, (8, 128), 1)
    at_low, at_high = lane == 0, lane == 127

    def after(x):
        return jnp.where(at_high, x, pltpu.roll(x, 127, 1))

    def before(x):
        return jnp.where(at_low, x, pltpu.roll(x, 1, 1))

    def layer(i, carry):
        at = first + i
        li = at + 2
        for r0 in rows:

            def load(dl, dr):
                return [cur[v, li + dl, pl.ds(r0 + dr, 8), :] for v in range(5)]

            mid = load(0, 0)
            near = [load(1, 0), load(-1, 0), load(0, 1), load(0, -1)]
            far = [load(2, 0), load(-2, 0), load(0, 2), load(0, -2)]
            fluxes = [half_flux(near[k], 1 + k // 2) for k in range(4)]
            radial = half_flux(mid, 3)
            for v in range(5):
                total = (fluxes[0][v] - fluxes[1][v]) + (fluxes[2][v] - fluxes[3][v])
                n1 = (near[0][v] + near[1][v]) + (near[2][v] + near[3][v])
                n2 = (far[0][v] + far[1][v]) + (far[2][v] + far[3][v])
                x = mid[v]
                eighth = 0.125 * x
                up = (eighth + radial[v]) - 0.03125 * after(x)
                down = (eighth - radial[v]) - 0.03125 * before(x)
                total = total + (after(up) + before(down)) + (0.125 * n1 - 0.03125 * n2)
                base = (1.0 + 8.0 * step) * flow[v, li, pl.ds(r0, 8), :] - (
                    2.0 * step
                ) * prior[v, at, pl.ds(r0, 8), :]
                new = base - (6.0 - 0.5625) * step * x - step * total
                out[v, at + out_offsets[0], pl.ds(r0 + out_offsets[1], 8), :] = new
        return carry

    if isinstance(count, int) and count == 2 and len(rows) == 1:
        lax.fori_loop(0, count, layer, 0, unroll=True)
    else:
        lax.fori_loop(0, count, layer, 0)


def sections_kernel(
    flow_hbm, prior_hbm, store_hbm, times_hbm, harm_hbm,
    state_out, store_out, ghosts_out,
    u0, u1, u2, prior, store, times, harm, share, ghosts, relay, faces, samples,
    local_sem, send_sem, recv_sem, word_sem,
):
    p = lax.axis_index("pitch")
    b = lax.axis_index("blk")
    n_blk = lax.axis_size("blk")
    last = lax.axis_size("pitch") - 1
    first_p, last_p = p == 0, p == last
    not_first, not_last = p > 0, p < last
    is_end = jnp.logical_or(first_p, last_p)
    b_low, b_high = b > 0, b < n_blk - 1
    above, below = {"pitch": p + 1}, {"pitch": p - 1}
    states = (u0, u1, u2)
    both = jnp.logical_and

    def signal(sem, where, cond):
        @pl.when(cond)
        def _():
            pl.semaphore_signal(sem, inc=1, device_id=where, device_id_type=MESH)

    def await_word(k, cond):
        @pl.when(cond)
        def _():
            pl.semaphore_wait(word_sem.at[k], 1)

    def number(cond):
        return cond.astype(jnp.int32)

    barrier = pltpu.get_barrier_semaphore()
    signal(barrier, above, not_last)
    signal(barrier, {"blk": b - 1}, b_low)
    signal(barrier, {"blk": b + 1}, b_high)
    signal(barrier, {"pitch": last}, first_p)
    signal(barrier, {"blk": b - 1, "pitch": last}, both(first_p, b_low))

    loads = [
        pltpu.make_async_copy(flow_hbm, u0.at[:, 2:10, 8:24, :], local_sem.at[0]),
        pltpu.make_async_copy(store_hbm.at[0], store.at[0], local_sem.at[1]),
        pltpu.make_async_copy(store_hbm.at[1], store.at[1], local_sem.at[2]),
        pltpu.make_async_copy(prior_hbm, prior.at[:, :, 8:24, :], local_sem.at[3]),
        pltpu.make_async_copy(times_hbm, times, local_sem.at[4]),
        pltpu.make_async_copy(harm_hbm, harm, local_sem.at[5]),
    ]
    for k in (0, 4, 5):
        loads[k].start()

    pl.semaphore_wait(
        barrier,
        number(not_first) + number(b_low) + number(b_high)
        + number(last_p) * (1 + number(b_high)),
    )
    signal(word_sem.at[0], below, not_first)
    signal(word_sem.at[1], {"pitch": 0}, last_p)

    sent = []

    def remote(src, dst, where, send_if, recv_if):
        k = len(sent)
        copy = pltpu.make_async_remote_copy(
            src_ref=src,
            dst_ref=dst,
            send_sem=send_sem.at[k],
            recv_sem=recv_sem.at[k],
            device_id=where,
            device_id_type=MESH,
        )
        sent.append((copy, send_if))
        return copy, send_if, recv_if

    def send(*copies):
        for copy, send_if, _ in copies:

            @pl.when(send_if)
            def _():
                copy.start()

    def arrive(*copies):
        for copy, _, recv_if in copies:

            @pl.when(recv_if)
            def _():
                copy.wait_recv()

    chunk_low = [lax.rem(b + t, 2) == 0 for t in range(2)]
    chunk_row = [pl.multiple_of(jnp.where(low, 8, 16), 8) for low in chunk_low]

    def pitch_copies(src, layer, shift, target):
        made = []
        for row in chunk_row:
            rows, there = pl.ds(pl.multiple_of(row - shift, 8), 8), pl.ds(row, 8)
            made.append(
                (
                    remote(
                        src.at[:, layer + 6 : layer + 8, rows, :], target.at[:, 0:2, there, :],
                        above, not_last, not_first,
                    ),
                    remote(
                        src.at[:, layer : layer + 2, rows, :], target.at[:, 10:12, there, :],
                        below, not_first, not_last,
                    ),
                )
            )
        return made

    pitch = [pitch_copies(flow_hbm, 0, 8, u0), pitch_copies(u1, 2, 0, u1), pitch_copies(u2, 2, 0, u2)]
    send(pitch[0][0][1], pitch[0][1][1])

    g6 = jnp.where(first_p, 0, 2)
    g4 = jnp.where(first_p, 0, 4)

    def beside(src, source, target, layers, count, shift, rows, cond, skip=0):
        there = pl.ds(layers + shift, count)
        here = pl.ds(layers + source[2], count)
        low, high = source[0], source[1]
        return (
            remote(
                src.at[:, here, high - skip - rows : high - skip, :],
                target.at[:, there, 8 - skip - rows : 8 - skip, :],
                {"blk": b + 1}, both(cond, b_high), both(cond, b_low),
            ),
            remote(
                src.at[:, here, low + skip : low + skip + rows, :],
                target.at[:, there, 24 + skip : 24 + skip + rows, :],
                {"blk": b - 1}, both(cond, b_low), both(cond, b_high),
            ),
        )

    plain, padded = (0, 16, 0), (8, 24, 2)
    flow_sides = beside(flow_hbm, plain, u0, 0, 8, 2, 2, p >= 0)
    flow_more = beside(flow_hbm, plain, u0, g6, 6, 2, 4, is_end, 2)
    prior_sides = beside(prior_hbm, plain, prior, g4, 4, 0, 4, is_end)
    send(*flow_sides)
    for k in (1, 2, 3):
        loads[k].start()

    def exchanged(s, q):
        ends = [0] if s == 1 else [0, 1]
        skip_first = both(first_p, jnp.asarray(q in ends))
        skip_last = both(last_p, jnp.asarray(3 - q in ends))
        return jnp.logical_not(jnp.logical_or(skip_first, skip_last))

    axial = {
        (s, q): beside(states[s], padded, states[s], 2 * q, 2, 2, 2, exchanged(s, q))
        for s in (1, 2)
        for q in range(4)
    }

    def outer_sides(s, t, wait, layers=(0, 3)):
        for q in layers:
            to_above, to_below = axial[s, q]
            for low in (True, False):
                copy, send_if, recv_if = to_below if low != wait else to_above
                cond = both(recv_if if wait else send_if, chunk_low[t] == low)

                @pl.when(cond)
                def _():
                    copy.wait_recv() if wait else copy.start()

    for k in (4, 5):
        loads[k].wait()
    count8 = twice(harm)
    for x in range(2):
        loads[1 + x].wait()
        turn = turned(base_turn(twice(times.at[x])), LAG if x else -LAG)

        def harmonic(k, carry):
            now, total = carry
            keep = k <= count8
            c, s = jnp.where(keep, now[0], 0.0), jnp.where(keep, now[1], 0.0)
            total = tuple(
                total[j]
                + (
                    store[x, k, 8 * j : 8 * j + 8, :] * c
                    + store[x, HARM + k, 8 * j : 8 * j + 8, :] * s
                )
                for j in range(5)
            )
            return times_turn(now, turn), total

        start = tuple(store[x, 0, 8 * j : 8 * j + 8, :] for j in range(5))
        _, total = lax.fori_loop(1, HARM + 1, harmonic, (turn, start))
        for j in range(5):
            share[x, 8 * j : 8 * j + 8, :] = total[j]

    low_early = [
        remote(share.at[0], ghosts.at[2], {"pitch": 0}, p == 1, first_p),
        remote(share.at[0], ghosts.at[4], {"pitch": 0}, last_p, first_p),
        remote(
            share.at[0], ghosts.at[0], {"blk": b + 1, "pitch": 0},
            both(last_p, b_high), both(first_p, b_low),
        ),
        remote(
            share.at[0], ghosts.at[5], {"blk": b - 1, "pitch": 0},
            both(first_p, b_low), both(first_p, b_high),
        ),
    ]
    low_later = remote(share.at[0], ghosts.at[3], {"pitch": 0}, p == 2, first_p)
    relayed = remote(share.at[1], relay.at[1], {"pitch": 0}, p == 1, first_p)
    high_early = remote(
        share.at[1], ghosts.at[0], {"blk": b + 1, "pitch": last},
        both(last_p, b_high), both(last_p, b_low),
    )
    high_next = remote(share.at[1], ghosts.at[3], {"pitch": last}, p == 2, last_p)
    high_relay = remote(relay, ghosts.at[1:3], {"pitch": last}, first_p, last_p)
    high_beside = remote(
        share.at[1], ghosts.at[5], {"blk": b - 1, "pitch": last},
        both(first_p, b_low), both(last_p, b_high),
    )
    send(*low_early, relayed, high_early, *flow_more, *prior_sides)

    await_word(0, not_last)
    send(pitch[0][0][0], pitch[0][1][0])
    signal(word_sem.at[2], above, jnp.logical_or(p == 1, p == 2))
    send(high_next)
    await_word(2, p == 2)
    send(low_later)

    def fill_edges(s, first, count):
        ref = states[s]
        for cond, row, source in ((b == 0, 6, 8), (b == n_blk - 1, 24, 23)):

            @pl.when(cond)
            def _():
                def layer(i, carry):
                    for v in range(5):
                        edge = ref[v, 2 + first + i, source : source + 1, :]
                        ref[v, 2 + first + i, row : row + 2, :] = jnp.broadcast_to(edge, (2, 128))
                    return carry

                lax.fori_loop(0, count, layer, 0)

    def update(s, first, count, rows):
        if s < 2:
            section(s, states[s], u0, prior, states[s + 1], (2, 0), first, count, rows)
        else:
            section(s, states[s], u0, prior, state_out, (0, -8), first, count, rows)

    def all_layers(s, between=None):
        fill_edges(s, 0, 8)
        if s == 0:
            update(0, 2, 4, CENTER)
            send(*axial[1, 1], *axial[1, 2])
        for t in range(2):
            if s > 0:
                outer_sides(s, t, True)
            for side, cond, first in ((0, not_first, 0), (1, not_last, 6)):

                @pl.when(cond)
                def _():
                    pitch[s][t][side][0].wait_recv()
                    update(s, first, 2, (chunk_row[t],))
                    if s < 2:
                        pitch[s + 1][t][1 - side][0].start()

                if s < 2:
                    outer_sides(s + 1, t, False, (3 * side,))
            if t == 0 and between:
                between()
            if t == 0 and s > 0:
                if s == 2:
                    arrive(*axial[s, 1], *axial[s, 2])
                if s == 1:
                    m2 = jnp.where(first_p, 4, 2)
                    update(s, jnp.where(is_end, m2, 2), jnp.where(is_end, 2, 4), CENTER)
                else:
                    update(s, 2, 4, CENTER)
                if s < 2:
                    send(*axial[s + 1, 1], *axial[s + 1, 2])

    loads[0].wait()
    loads[3].wait()
    arrive(*flow_sides)
    all_layers(0)

    @pl.when(first_p)
    def _():
        pl.semaphore_wait(word_sem.at[1], 1)
        relay[0] = share[1]
        relayed[0].wait_recv()
        high_relay[0].start()

    send(high_beside)
    face_copies = []
    for x, source in ((0, 3), (1, 0)):
        for j in range(4):
            if j != source:
                face_copies.append(
                    remote(faces.at[j], samples.at[x], {"pitch": j}, p == source, p == j)
                )

    def ghosts_chain():
        @pl.when(is_end)
        def _():
            arrive(*flow_more, *prior_sides, *low_early, low_later, high_early, high_next, high_relay, high_beside)
            pl.when(first_p)(lambda: ghosts.__setitem__(1, share[0]))
            pl.when(last_p)(lambda: ghosts.__setitem__(4, share[1]))
            outside = jnp.where(first_p, 0, 10)
            for k in range(6):

                @pl.when(b_low if k == 0 else (b_high if k == 5 else is_end))
                def _():
                    for v in range(5):
                        for layer in range(2):
                            at = (2 * v + layer) * 4
                            block = ghosts[k, at : at + 4, :]
                            for ref in states:
                                ref[v, outside + layer, 4 + 4 * k : 8 + 4 * k, :] = block

            for q, mine in ((1, first_p), (2, last_p)):
                for copy, send_if, _ in axial[1, q]:

                    @pl.when(both(send_if, mine))
                    def _():
                        copy.wait_send()

            near = jnp.where(first_p, 0, 6)
            update(0, g4, 4, EXTENDED)
            fill_edges(1, g4, 4)
            update(1, g4, 4, EXTENDED)
            fill_edges(2, g4, 4)
            update(2, near, 2, CENTER)
            for j in range(4):
                for v in range(5):
                    for layer in range(2):
                        at = (2 * v + layer) * 4
                        faces[j, at : at + 4, :] = state_out[v, near + layer, 4 * j : 4 * j + 4, :]

        await_word(2, last_p)
        send(*face_copies)
        pl.when(first_p)(lambda: samples.__setitem__(1, faces[0]))
        pl.when(last_p)(lambda: samples.__setitem__(0, faces[3]))

    arrive(*axial[1, 1], *axial[1, 2])
    ghosts_chain()
    all_layers(1)
    def refresh():
        arrive(*face_copies)
        for x in range(2):
            turn = turned(base_turn(twice(times.at[x])), PERIOD)
            lagged = turned(turn, LAG if x else -LAG)
            seen = tuple(samples[x, 8 * j : 8 * j + 8, :] for j in range(5))
            total = tuple(
                0.875 * store[x, 0, 8 * j : 8 * j + 8, :] + 0.125 * seen[j] for j in range(5)
            )
            for j in range(5):
                store_out[x, 0, 8 * j : 8 * j + 8, :] = total[j]

            def harmonic(k, carry):
                now, late, total = carry
                keep = k <= count8
                c, s = jnp.where(keep, late[0], 0.0), jnp.where(keep, late[1], 0.0)
                wc, ws = 0.25 * now[0], 0.25 * now[1]
                sums = []
                for j in range(5):
                    rows = slice(8 * j, 8 * j + 8)
                    new_c = 0.875 * store[x, k, rows, :] + wc * seen[j]
                    new_s = 0.875 * store[x, HARM + k, rows, :] + ws * seen[j]
                    store_out[x, k, rows, :] = new_c
                    store_out[x, HARM + k, rows, :] = new_s
                    sums.append(total[j] + (new_c * c + new_s * s))
                return times_turn(now, turn), times_turn(late, lagged), tuple(sums)

            carry = lax.fori_loop(1, HARM + 1, harmonic, (turn, lagged, total), unroll=2)
            for j in range(5):
                ghosts_out[x, 8 * j : 8 * j + 8, :] = carry[2][j]

    all_layers(2, refresh)
    early = [(axial[1, 1], first_p), (axial[1, 2], last_p)]
    for copy, cond in sent:
        for copies, mine in early:
            if any(copy is made[0] for made in copies):
                cond = both(cond, jnp.logical_not(mine))

        @pl.when(cond)
        def _():
            copy.wait_send()


def finish_kernel(state, store, ghosts, state_out, store_out, ghosts_out, sems):
    copies = [
        pltpu.make_async_copy(store.at[0], store_out.at[0], sems.at[0]),
        pltpu.make_async_copy(store.at[1], store_out.at[1], sems.at[1]),
        pltpu.make_async_copy(state, state_out, sems.at[2]),
        pltpu.make_async_copy(ghosts, ghosts_out, sems.at[3]),
    ]
    for copy in copies:
        copy.start()
    for copy in copies:
        copy.wait()


def shards(flow_state, prior_state, fourier_store, sample_times, harmonics):
    cells = flow_state.shape
    store_flat = fourier_store.reshape(2, COEFS, 40, 128)
    anywhere = pl.BlockSpec(memory_space=pl.ANY)
    vmem = pl.BlockSpec(memory_space=pltpu.VMEM)
    state, fresh, seen = pl.pallas_call(
        sections_kernel,
        out_shape=(
            jax.ShapeDtypeStruct(cells, F32),
            jax.ShapeDtypeStruct(store_flat.shape, F32),
            jax.ShapeDtypeStruct((2, 40, 128), F32),
        ),
        in_specs=[pl.BlockSpec(memory_space=pltpu.HBM)] * 5,
        out_specs=(vmem, vmem, vmem),
        scratch_shapes=[
            pltpu.VMEM((5, 12, 32, 128), F32),
            pltpu.VMEM((5, 12, 32, 128), F32),
            pltpu.VMEM((5, 12, 32, 128), F32),
            pltpu.VMEM((5, 8, 32, 128), F32),
            pltpu.VMEM((2, COEFS, 40, 128), F32),
            pltpu.VMEM((2, 4, 128), jnp.int32),
            pltpu.VMEM((4, 128), jnp.int32),
            pltpu.VMEM((2, 40, 128), F32),
            pltpu.VMEM((6, 40, 128), F32),
            pltpu.VMEM((2, 40, 128), F32),
            pltpu.VMEM((4, 40, 128), F32),
            pltpu.VMEM((2, 40, 128), F32),
            pltpu.SemaphoreType.DMA((6,)),
            pltpu.SemaphoreType.DMA((64,)),
            pltpu.SemaphoreType.DMA((64,)),
            pltpu.SemaphoreType.REGULAR((3,)),
        ],
        compiler_params=pltpu.CompilerParams(
            collective_id=0, has_side_effects=True, vmem_limit_bytes=24 * 1024 * 1024
        ),
        name="sections",
    )(*[pltpu.with_memory_space_constraint(x, pltpu.HBM) for x in (flow_state, prior_state, store_flat, sample_times, harmonics)])
    new_state, new_store, ghosts = pl.pallas_call(
        finish_kernel,
        out_shape=(
            jax.ShapeDtypeStruct(cells, F32),
            jax.ShapeDtypeStruct(store_flat.shape, F32),
            jax.ShapeDtypeStruct((2, 40, 128), F32),
        ),
        in_specs=[vmem] * 3,
        out_specs=(anywhere,) * 3,
        scratch_shapes=[pltpu.SemaphoreType.DMA((4,))],
        name="finish",
    )(*[pltpu.with_memory_space_constraint(x, pltpu.VMEM) for x in (state, fresh, seen)])
    return (
        new_state,
        new_store.reshape(fourier_store.shape),
        ghosts.reshape(2, 10, 4, 128),
    )


def solution(mesh):
    placed = (
        P(None, "pitch", "blk", None),
        P(None, "pitch", "blk", None),
        P(None, None, None, ("blk", "pitch"), None),
        P(None, ("blk", "pitch"), None),
        P(("blk", "pitch"), None),
    )
    return jax.shard_map(
        shards,
        mesh=mesh,
        in_specs=placed,
        out_specs=(
            P(None, "pitch", "blk", None),
            P(None, None, None, ("blk", "pitch"), None),
            P(None, None, ("blk", "pitch"), None),
        ),
        check_vma=False,
    )
```

```python
import functools
import math

import jax
import jax.numpy as jnp
from jax import lax
from jax.experimental import pallas as pl
from jax.experimental.pallas import tpu as pltpu
from jax.sharding import PartitionSpec as P

MESH = pl.DeviceIdType.MESH
F32 = jnp.float32
NT = 96
HARM = 24
COEFS = 2 * HARM + 1
PERIOD = 2.0 * math.pi / NT
LAG = 2.0 * math.pi * 0.3
SECTIONS = (1.0 / 3.0, 0.5, 1.0)
CENTER = (8, 16)
EXTENDED = (4, 12, 20)


def twice(ref):
    rows = ref[...]
    return jnp.concatenate([rows, rows], axis=0)


def base_turn(times):
    quarter = (times - NT // 2).astype(F32) * (PERIOD / 4.0)
    sq = quarter * quarter
    s = quarter * (1.0 + sq * (-1.0 / 6 + sq * (1.0 / 120 + sq * (-1.0 / 5040 + sq * (1.0 / 362880)))))
    c = 1.0 + sq * (
        -0.5 + sq * (1.0 / 24 + sq * (-1.0 / 720 + sq * (1.0 / 40320 + sq * (-1.0 / 3628800))))
    )
    for _ in range(2):
        c, s = 1.0 - 2.0 * s * s, 2.0 * s * c
    return -c, -s


def turned(turn, angle):
    c, s = turn
    ca, sa = math.cos(angle), math.sin(angle)
    return c * ca - s * sa, s * ca + c * sa


def times_turn(a, b):
    return a[0] * b[0] - a[1] * b[1], a[1] * b[0] + a[0] * b[1]


def half_flux(cell, direction):
    rho, mp, ma, mr, energy = cell
    inv = pl.reciprocal(rho, approx=True)
    half_inv = inv * (1.0 - (0.5 * rho) * inv)
    kinetic = (mp * mp + ma * ma + mr * mr) * half_inv
    half_p = 0.2 * (energy - kinetic)
    moment = cell[direction]
    half_u = moment * half_inv
    parts = [
        0.5 * moment,
        mp * half_u,
        ma * half_u,
        mr * half_u,
        (energy + (half_p + half_p)) * half_u,
    ]
    parts[direction] = parts[direction] + half_p
    return parts


def section(s, cur, flow, prior, out, out_offsets, first, count, rows):
    step = 0.1 * SECTIONS[s]
    lane = lax.broadcasted_iota(jnp.int32, (8, 128), 1)
    at_low, at_high = lane == 0, lane == 127

    def after(x):
        return jnp.where(at_high, x, pltpu.roll(x, 127, 1))

    def before(x):
        return jnp.where(at_low, x, pltpu.roll(x, 1, 1))

    def layer(i, carry):
        at = first + i
        li = at + 2
        for r0 in rows:

            def load(dl, dr):
                return [cur[v, li + dl, pl.ds(r0 + dr, 8), :] for v in range(5)]

            mid = load(0, 0)
            near = [load(1, 0), load(-1, 0), load(0, 1), load(0, -1)]
            far = [load(2, 0), load(-2, 0), load(0, 2), load(0, -2)]
            fluxes = [half_flux(near[k], 1 + k // 2) for k in range(4)]
            radial = half_flux(mid, 3)
            for v in range(5):
                total = (fluxes[0][v] - fluxes[1][v]) + (fluxes[2][v] - fluxes[3][v])
                n1 = (near[0][v] + near[1][v]) + (near[2][v] + near[3][v])
                n2 = (far[0][v] + far[1][v]) + (far[2][v] + far[3][v])
                x = mid[v]
                eighth = 0.125 * x
                up = (eighth + radial[v]) - 0.03125 * after(x)
                down = (eighth - radial[v]) - 0.03125 * before(x)
                total = total + (after(up) + before(down)) + (0.125 * n1 - 0.03125 * n2)
                base = (1.0 + 8.0 * step) * flow[v, li, pl.ds(r0, 8), :] - (
                    2.0 * step
                ) * prior[v, at, pl.ds(r0, 8), :]
                new = base - (6.0 - 0.5625) * step * x - step * total
                out[v, at + out_offsets[0], pl.ds(r0 + out_offsets[1], 8), :] = new
        return carry

    if isinstance(count, int) and count == 2 and len(rows) == 1:
        lax.fori_loop(0, count, layer, 0, unroll=True)
    else:
        lax.fori_loop(0, count, layer, 0)


def sections_kernel(
    flow_hbm, prior_hbm, store_hbm, times_hbm, harm_hbm,
    state_out, store_out, ghosts_out,
    u0, u1, u2, prior, store, times, harm, share, ghosts, relay, faces, samples,
    local_sem, send_sem, recv_sem, word_sem,
):
    p = lax.axis_index("pitch")
    b = lax.axis_index("blk")
    n_blk = lax.axis_size("blk")
    last = lax.axis_size("pitch") - 1
    first_p, last_p = p == 0, p == last
    not_first, not_last = p > 0, p < last
    is_end = jnp.logical_or(first_p, last_p)
    b_low, b_high = b > 0, b < n_blk - 1
    above, below = {"pitch": p + 1}, {"pitch": p - 1}
    states = (u0, u1, u2)
    both = jnp.logical_and

    def signal(sem, where, cond):
        @pl.when(cond)
        def _():
            pl.semaphore_signal(sem, inc=1, device_id=where, device_id_type=MESH)

    def await_word(k, cond):
        @pl.when(cond)
        def _():
            pl.semaphore_wait(word_sem.at[k], 1)

    def number(cond):
        return cond.astype(jnp.int32)

    barrier = pltpu.get_barrier_semaphore()
    signal(barrier, above, not_last)
    signal(barrier, {"blk": b - 1}, b_low)
    signal(barrier, {"blk": b + 1}, b_high)
    signal(barrier, {"pitch": last}, first_p)
    signal(barrier, {"blk": b - 1, "pitch": last}, both(first_p, b_low))

    loads = [
        pltpu.make_async_copy(flow_hbm, u0.at[:, 2:10, 8:24, :], local_sem.at[0]),
        pltpu.make_async_copy(store_hbm.at[0], store.at[0], local_sem.at[1]),
        pltpu.make_async_copy(store_hbm.at[1], store.at[1], local_sem.at[2]),
        pltpu.make_async_copy(prior_hbm, prior.at[:, :, 8:24, :], local_sem.at[3]),
        pltpu.make_async_copy(times_hbm, times, local_sem.at[4]),
        pltpu.make_async_copy(harm_hbm, harm, local_sem.at[5]),
    ]
    for k in (0, 4, 5):
        loads[k].start()

    pl.semaphore_wait(
        barrier,
        number(not_first) + number(b_low) + number(b_high)
        + number(last_p) * (1 + number(b_high)),
    )
    signal(word_sem.at[0], below, not_first)
    signal(word_sem.at[1], {"pitch": 0}, last_p)

    sent = []

    def remote(src, dst, where, send_if, recv_if):
        k = len(sent)
        copy = pltpu.make_async_remote_copy(
            src_ref=src,
            dst_ref=dst,
            send_sem=send_sem.at[k],
            recv_sem=recv_sem.at[k],
            device_id=where,
            device_id_type=MESH,
        )
        sent.append((copy, send_if))
        return copy, send_if, recv_if

    def send(*copies):
        for copy, send_if, _ in copies:

            @pl.when(send_if)
            def _():
                copy.start()

    def arrive(*copies):
        for copy, _, recv_if in copies:

            @pl.when(recv_if)
            def _():
                copy.wait_recv()

    chunk_low = [lax.rem(b + t, 2) == 0 for t in range(2)]
    chunk_row = [pl.multiple_of(jnp.where(low, 8, 16), 8) for low in chunk_low]

    def pitch_copies(src, layer, shift, target):
        made = []
        for row in chunk_row:
            rows, there = pl.ds(pl.multiple_of(row - shift, 8), 8), pl.ds(row, 8)
            made.append(
                (
                    remote(
                        src.at[:, layer + 6 : layer + 8, rows, :], target.at[:, 0:2, there, :],
                        above, not_last, not_first,
                    ),
                    remote(
                        src.at[:, layer : layer + 2, rows, :], target.at[:, 10:12, there, :],
                        below, not_first, not_last,
                    ),
                )
            )
        return made

    pitch = [pitch_copies(flow_hbm, 0, 8, u0), pitch_copies(u1, 2, 0, u1), pitch_copies(u2, 2, 0, u2)]
    send(pitch[0][0][1], pitch[0][1][1])

    g6 = jnp.where(first_p, 0, 2)
    g4 = jnp.where(first_p, 0, 4)

    def beside(src, source, target, layers, count, shift, rows, cond, skip=0):
        there = pl.ds(layers + shift, count)
        here = pl.ds(layers + source[2], count)
        low, high = source[0], source[1]
        return (
            remote(
                src.at[:, here, high - skip - rows : high - skip, :],
                target.at[:, there, 8 - skip - rows : 8 - skip, :],
                {"blk": b + 1}, both(cond, b_high), both(cond, b_low),
            ),
            remote(
                src.at[:, here, low + skip : low + skip + rows, :],
                target.at[:, there, 24 + skip : 24 + skip + rows, :],
                {"blk": b - 1}, both(cond, b_low), both(cond, b_high),
            ),
        )

    plain, padded = (0, 16, 0), (8, 24, 2)
    flow_sides = beside(flow_hbm, plain, u0, 0, 8, 2, 2, p >= 0)
    flow_more = beside(flow_hbm, plain, u0, g6, 6, 2, 4, is_end, 2)
    prior_sides = beside(prior_hbm, plain, prior, g4, 4, 0, 4, is_end)
    send(*flow_sides)
    for k in (1, 2, 3):
        loads[k].start()

    def exchanged(s, q):
        ends = [0] if s == 1 else [0, 1]
        skip_first = both(first_p, jnp.asarray(q in ends))
        skip_last = both(last_p, jnp.asarray(3 - q in ends))
        return jnp.logical_not(jnp.logical_or(skip_first, skip_last))

    axial = {
        (s, q): beside(states[s], padded, states[s], 2 * q, 2, 2, 2, exchanged(s, q))
        for s in (1, 2)
        for q in range(4)
    }

    def outer_sides(s, t, wait, layers=(0, 3)):
        for q in layers:
            to_above, to_below = axial[s, q]
            for low in (True, False):
                copy, send_if, recv_if = to_below if low != wait else to_above
                cond = both(recv_if if wait else send_if, chunk_low[t] == low)

                @pl.when(cond)
                def _():
                    copy.wait_recv() if wait else copy.start()

    for k in (4, 5):
        loads[k].wait()
    count8 = twice(harm)
    for x in range(2):
        loads[1 + x].wait()
        turn = turned(base_turn(twice(times.at[x])), LAG if x else -LAG)

        def harmonic(k, carry):
            now, total = carry
            keep = k <= count8
            c, s = jnp.where(keep, now[0], 0.0), jnp.where(keep, now[1], 0.0)
            total = tuple(
                total[j]
                + (
                    store[x, k, 8 * j : 8 * j + 8, :] * c
                    + store[x, HARM + k, 8 * j : 8 * j + 8, :] * s
                )
                for j in range(5)
            )
            return times_turn(now, turn), total

        start = tuple(store[x, 0, 8 * j : 8 * j + 8, :] for j in range(5))
        _, total = lax.fori_loop(1, HARM + 1, harmonic, (turn, start))
        for j in range(5):
            share[x, 8 * j : 8 * j + 8, :] = total[j]

    low_early = [
        remote(share.at[0], ghosts.at[2], {"pitch": 0}, p == 1, first_p),
        remote(share.at[0], ghosts.at[4], {"pitch": 0}, last_p, first_p),
        remote(
            share.at[0], ghosts.at[0], {"blk": b + 1, "pitch": 0},
            both(last_p, b_high), both(first_p, b_low),
        ),
        remote(
            share.at[0], ghosts.at[5], {"blk": b - 1, "pitch": 0},
            both(first_p, b_low), both(first_p, b_high),
        ),
    ]
    low_later = remote(share.at[0], ghosts.at[3], {"pitch": 0}, p == 2, first_p)
    relayed = remote(share.at[1], relay.at[1], {"pitch": 0}, p == 1, first_p)
    high_early = remote(
        share.at[1], ghosts.at[0], {"blk": b + 1, "pitch": last},
        both(last_p, b_high), both(last_p, b_low),
    )
    high_next = remote(share.at[1], ghosts.at[3], {"pitch": last}, p == 2, last_p)
    high_relay = remote(relay, ghosts.at[1:3], {"pitch": last}, first_p, last_p)
    high_beside = remote(
        share.at[1], ghosts.at[5], {"blk": b - 1, "pitch": last},
        both(first_p, b_low), both(last_p, b_high),
    )
    send(*low_early, relayed, high_early, *flow_more, *prior_sides)

    await_word(0, not_last)
    send(pitch[0][0][0], pitch[0][1][0])
    signal(word_sem.at[2], above, jnp.logical_or(p == 1, p == 2))
    send(high_next)
    await_word(2, p == 2)
    send(low_later)

    def fill_edges(s, first, count):
        ref = states[s]
        for cond, row, source in ((b == 0, 6, 8), (b == n_blk - 1, 24, 23)):

            @pl.when(cond)
            def _():
                def layer(i, carry):
                    for v in range(5):
                        edge = ref[v, 2 + first + i, source : source + 1, :]
                        ref[v, 2 + first + i, row : row + 2, :] = jnp.broadcast_to(edge, (2, 128))
                    return carry

                lax.fori_loop(0, count, layer, 0)

    def update(s, first, count, rows):
        if s < 2:
            section(s, states[s], u0, prior, states[s + 1], (2, 0), first, count, rows)
        else:
            section(s, states[s], u0, prior, state_out, (0, -8), first, count, rows)

    def all_layers(s, between=None):
        fill_edges(s, 0, 8)
        if s == 0:
            update(0, 2, 4, CENTER)
            send(*axial[1, 1], *axial[1, 2])
        for t in range(2):
            if s > 0:
                outer_sides(s, t, True)
            for side, cond, first in ((0, not_first, 0), (1, not_last, 6)):

                @pl.when(cond)
                def _():
                    pitch[s][t][side][0].wait_recv()
                    update(s, first, 2, (chunk_row[t],))
                    if s < 2:
                        pitch[s + 1][t][1 - side][0].start()

                if s < 2:
                    outer_sides(s + 1, t, False, (3 * side,))
            if t == 0 and s > 0:
                if s == 2:
                    arrive(*axial[s, 1], *axial[s, 2])
                if s == 1:
                    m2 = jnp.where(first_p, 4, 2)
                    update(s, jnp.where(is_end, m2, 2), jnp.where(is_end, 2, 4), CENTER)
                else:
                    update(s, 2, 4, CENTER)
                if s < 2:
                    send(*axial[s + 1, 1], *axial[s + 1, 2])
                if between:
                    between()

    loads[0].wait()
    loads[3].wait()
    arrive(*flow_sides)
    all_layers(0)

    @pl.when(first_p)
    def _():
        pl.semaphore_wait(word_sem.at[1], 1)
        relay[0] = share[1]
        relayed[0].wait_recv()
        high_relay[0].start()

    send(high_beside)
    face_copies = []
    for x, source in ((0, 3), (1, 0)):
        for j in range(4):
            if j != source:
                face_copies.append(
                    remote(faces.at[j], samples.at[x], {"pitch": j}, p == source, p == j)
                )

    def ghosts_chain():
        @pl.when(is_end)
        def _():
            arrive(*flow_more, *prior_sides, *low_early, low_later, high_early, high_next, high_relay, high_beside)
            pl.when(first_p)(lambda: ghosts.__setitem__(1, share[0]))
            pl.when(last_p)(lambda: ghosts.__setitem__(4, share[1]))
            outside = jnp.where(first_p, 0, 10)
            for k in range(6):

                @pl.when(b_low if k == 0 else (b_high if k == 5 else is_end))
                def _():
                    for v in range(5):
                        for layer in range(2):
                            at = (2 * v + layer) * 4
                            block = ghosts[k, at : at + 4, :]
                            for ref in states:
                                ref[v, outside + layer, 4 + 4 * k : 8 + 4 * k, :] = block

            for q, mine in ((1, first_p), (2, last_p)):
                for copy, send_if, _ in axial[1, q]:

                    @pl.when(both(send_if, mine))
                    def _():
                        copy.wait_send()

            near = jnp.where(first_p, 0, 6)
            update(0, g4, 4, EXTENDED)
            fill_edges(1, g4, 4)
            update(1, g4, 4, EXTENDED)
            fill_edges(2, g4, 4)
            update(2, near, 2, CENTER)
            for j in range(4):
                for v in range(5):
                    for layer in range(2):
                        at = (2 * v + layer) * 4
                        faces[j, at : at + 4, :] = state_out[v, near + layer, 4 * j : 4 * j + 4, :]

        await_word(2, last_p)
        send(*face_copies)
        pl.when(first_p)(lambda: samples.__setitem__(1, faces[0]))
        pl.when(last_p)(lambda: samples.__setitem__(0, faces[3]))

    arrive(*axial[1, 1], *axial[1, 2])
    ghosts_chain()
    all_layers(1)
    def refresh():
        arrive(*face_copies)
        for x in range(2):
            turn = turned(base_turn(twice(times.at[x])), PERIOD)
            lagged = turned(turn, LAG if x else -LAG)
            seen = tuple(samples[x, 8 * j : 8 * j + 8, :] for j in range(5))
            total = tuple(
                0.875 * store[x, 0, 8 * j : 8 * j + 8, :] + 0.125 * seen[j] for j in range(5)
            )
            for j in range(5):
                store_out[x, 0, 8 * j : 8 * j + 8, :] = total[j]

            def harmonic(k, carry):
                now, late, total = carry
                keep = k <= count8
                c, s = jnp.where(keep, late[0], 0.0), jnp.where(keep, late[1], 0.0)
                wc, ws = 0.25 * now[0], 0.25 * now[1]
                sums = []
                for j in range(5):
                    rows = slice(8 * j, 8 * j + 8)
                    new_c = 0.875 * store[x, k, rows, :] + wc * seen[j]
                    new_s = 0.875 * store[x, HARM + k, rows, :] + ws * seen[j]
                    store_out[x, k, rows, :] = new_c
                    store_out[x, HARM + k, rows, :] = new_s
                    sums.append(total[j] + (new_c * c + new_s * s))
                return times_turn(now, turn), times_turn(late, lagged), tuple(sums)

            carry = lax.fori_loop(1, HARM + 1, harmonic, (turn, lagged, total), unroll=2)
            for j in range(5):
                ghosts_out[x, 8 * j : 8 * j + 8, :] = carry[2][j]

    all_layers(2, refresh)
    early = [(axial[1, 1], first_p), (axial[1, 2], last_p)]
    for copy, cond in sent:
        for copies, mine in early:
            if any(copy is made[0] for made in copies):
                cond = both(cond, jnp.logical_not(mine))

        @pl.when(cond)
        def _():
            copy.wait_send()


def finish_kernel(state, store, ghosts, state_out, store_out, ghosts_out, sems):
    copies = [
        pltpu.make_async_copy(store.at[0], store_out.at[0], sems.at[0]),
        pltpu.make_async_copy(store.at[1], store_out.at[1], sems.at[1]),
        pltpu.make_async_copy(state, state_out, sems.at[2]),
        pltpu.make_async_copy(ghosts, ghosts_out, sems.at[3]),
    ]
    for copy in copies:
        copy.start()
    for copy in copies:
        copy.wait()


def shards(flow_state, prior_state, fourier_store, sample_times, harmonics):
    cells = flow_state.shape
    store_flat = fourier_store.reshape(2, COEFS, 40, 128)
    anywhere = pl.BlockSpec(memory_space=pl.ANY)
    vmem = pl.BlockSpec(memory_space=pltpu.VMEM)
    state, fresh, seen = pl.pallas_call(
        sections_kernel,
        out_shape=(
            jax.ShapeDtypeStruct(cells, F32),
            jax.ShapeDtypeStruct(store_flat.shape, F32),
            jax.ShapeDtypeStruct((2, 40, 128), F32),
        ),
        in_specs=[pl.BlockSpec(memory_space=pltpu.HBM)] * 5,
        out_specs=(vmem, vmem, vmem),
        scratch_shapes=[
            pltpu.VMEM((5, 12, 32, 128), F32),
            pltpu.VMEM((5, 12, 32, 128), F32),
            pltpu.VMEM((5, 12, 32, 128), F32),
            pltpu.VMEM((5, 8, 32, 128), F32),
            pltpu.VMEM((2, COEFS, 40, 128), F32),
            pltpu.VMEM((2, 4, 128), jnp.int32),
            pltpu.VMEM((4, 128), jnp.int32),
            pltpu.VMEM((2, 40, 128), F32),
            pltpu.VMEM((6, 40, 128), F32),
            pltpu.VMEM((2, 40, 128), F32),
            pltpu.VMEM((4, 40, 128), F32),
            pltpu.VMEM((2, 40, 128), F32),
            pltpu.SemaphoreType.DMA((6,)),
            pltpu.SemaphoreType.DMA((64,)),
            pltpu.SemaphoreType.DMA((64,)),
            pltpu.SemaphoreType.REGULAR((3,)),
        ],
        compiler_params=pltpu.CompilerParams(
            collective_id=0, has_side_effects=True, vmem_limit_bytes=24 * 1024 * 1024
        ),
        name="sections",
    )(*[pltpu.with_memory_space_constraint(x, pltpu.HBM) for x in (flow_state, prior_state, store_flat, sample_times, harmonics)])
    new_state, new_store, ghosts = pl.pallas_call(
        finish_kernel,
        out_shape=(
            jax.ShapeDtypeStruct(cells, F32),
            jax.ShapeDtypeStruct(store_flat.shape, F32),
            jax.ShapeDtypeStruct((2, 40, 128), F32),
        ),
        in_specs=[vmem] * 3,
        out_specs=(anywhere,) * 3,
        scratch_shapes=[pltpu.SemaphoreType.DMA((4,))],
        name="finish",
    )(*[pltpu.with_memory_space_constraint(x, pltpu.VMEM) for x in (state, fresh, seen)])
    return (
        new_state,
        new_store.reshape(fourier_store.shape),
        ghosts.reshape(2, 10, 4, 128),
    )


def solution(mesh):
    placed = (
        P(None, "pitch", "blk", None),
        P(None, "pitch", "blk", None),
        P(None, None, None, ("blk", "pitch"), None),
        P(None, ("blk", "pitch"), None),
        P(("blk", "pitch"), None),
    )
    return jax.shard_map(
        shards,
        mesh=mesh,
        in_specs=placed,
        out_specs=(
            P(None, "pitch", "blk", None),
            P(None, None, None, ("blk", "pitch"), None),
            P(None, None, ("blk", "pitch"), None),
        ),
        check_vma=False,
    )
```
